128 devices in a mesh: sample: 32 (over x, z, core), feature: 4 (over y).
Axes of the slice: x: 4, y: 4, z: 4, core: 2. Of those that a mesh axis runs over, the one named last changes fastest.
Arguments:
- feat_values: float32 [65536, 2048], P('sample', 'feature'), may hold values from -0.6 to 0.6
- block_ids: int32 [512, 16], P('sample', 'feature'), may hold values from 0 to 8191
- fixed_weights: float32 [32768, 128], P('feature'), may hold values from -1.5 to 1.5
- labels: float32 [65536], P('sample'), may hold values from 0 to 1
- prior_scores: float32 [65536], P('sample'), may hold values from -3 to 3
- member_feats: float32 [65536, 128], P(('sample', 'feature')), may hold values from -1.8 to 1.8
- member_ids: int32 [65536], P(('sample', 'feature')), may hold values from 0 to 4095, as said below
- member_coefs: float32 [4096, 128], P(('sample', 'feature')), may hold values from -1.5 to 1.5
Outputs:
- new_weights: float32 [32768, 128], P('feature')
- new_coefs: float32 [4096, 128], P(('sample', 'feature'))
- total_scores: float32 [65536, 1], P(('sample', 'feature'))
The draws below stay inside these ranges and needn't reach their ends.
Inputs may be any that keep to these rules, and one draw needn't show every extreme that they name: member_ids // 32 is the index along sample+feature of the device that owns the member; no member has more than 32 rows, and every member of some owner has exactly 32; at most 8 rows of one device belong to members of one owner, and every device has exactly 8 rows for some owner.
All inputs are finite; a program needn't handle non-finite values.
Results may differ from the reference program's by a relative error of at most 0.0003.
Values sent between devices are 32-bit elements; how exact they have to be, the bound alone decides.
No kernel may reach another device: no remote copies, remote signals or barrier semaphores. Data moves between devices by JAX's collectives and lax.ppermute only.
A program may use at most 128 MiB of HBM per device.

```python
import math
import jax
import jax.numpy as jnp
from jax import lax

BLK = 128
FEAT_BLOCKS = 32768
KB = 4
TILE = 128
RE_FEAT = 128
NEWTON = 2
MEM_DEV = 32
ROWS = 65536
RE_DEV = 512
MEMBERS = 4096
CAP = 8
N_SAMPLE = 32
N_FEATURE = 4


def route_table(key):
    senders = N_SAMPLE * N_FEATURE
    slots_all = senders * CAP
    group_rows = slots_all // MEM_DEV
    base = jax.random.fold_in(key, 7)
    keys = jax.random.split(base, senders)
    filled = jax.random.randint(jax.random.fold_in(base, 11), (), 0, senders)
    owner_keys = jax.random.split(jax.random.fold_in(base, 13), senders)
    tables = jax.vmap(lambda sub: jax.random.permutation(sub, slots_all).astype(jnp.int32))(owner_keys)
    sender_index = jnp.arange(senders, dtype=jnp.int32)

    def single(sub, source):
        second = jax.random.fold_in(sub, 3)
        position = jnp.arange(slots_all, dtype=jnp.int32)
        ranking = jax.random.permutation(second, slots_all).astype(jnp.int32)
        scores = jnp.where(position // CAP == filled, position, slots_all + ranking)
        order = jnp.argsort(scores, stable=True).astype(jnp.int32)
        chosen = order[:RE_DEV]
        owner = chosen // CAP
        arrival = source * CAP + chosen % CAP
        local = tables[owner, arrival] // group_rows
        return (chosen, owner * MEM_DEV + local)
    slots, members = jax.vmap(single)(keys, sender_index)
    return members.reshape(-1).astype(jnp.int32)


def draw_member_ids(key, part):
    return route_table(key)


def set_ends(array, key, least, largest):
    longest = array.shape.index(max(array.shape))
    spots = []
    for shift in (0, 1):
        where = [jax.random.randint(jax.random.fold_in(key, axis), (), 0, length) for axis, length in enumerate(array.shape)]
        where[longest] = (where[longest] + shift) % array.shape[longest]
        spots.append(tuple(where))
    return array.at[spots[0]].set(least).at[spots[1]].set(largest)


def shard_levels(key, extent, cuts, smallest, high):
    loudness = 1.0
    for dim, shards_of in cuts:
        steps = jax.random.uniform(jax.random.fold_in(jax.random.fold_in(key, 6), dim), (shards_of,), jnp.float32, smallest / len(cuts), high / len(cuts))
        loudness = loudness * jnp.repeat(jnp.exp(steps), extent[dim] // shards_of).reshape((-1,) + (1,) * (len(extent) - 1 - dim))
    return loudness


def bell_draw(key, extent, spread, limit, cuts=(), kind=jnp.bfloat16):
    array = spread * jax.random.normal(key, extent, jnp.float32)
    if cuts:
        array = array * shard_levels(key, extent, cuts, -0.22, 0.18)
    return jnp.clip(array, -limit, limit).astype(kind)


def setup_inputs(seed: int = 0) -> dict:
    key_of = jax.random.split(jax.random.key(seed), 9)
    feat_values = bell_draw(key_of[0], (ROWS, N_FEATURE * KB * BLK), 0.1, 0.6, ((0, 32), (1, 4)), jnp.float32)
    block_ids = set_ends(jax.random.randint(key_of[1], (ROWS // TILE, N_FEATURE * KB), 0, FEAT_BLOCKS // N_FEATURE), jax.random.fold_in(key_of[1], 1), 0, (FEAT_BLOCKS // N_FEATURE) - 1).astype(jnp.int32)
    fixed_weights = bell_draw(key_of[2], (FEAT_BLOCKS, BLK), 0.25, 1.5, ((0, 4),), jnp.float32)
    labels = jnp.clip(1.0 * jax.random.uniform(key_of[3], (ROWS,), jnp.float32) ** shard_levels(key_of[3], (ROWS,), ((0, 32),), -0.2, 0.2), 0.0, 1.0)
    prior_scores = bell_draw(key_of[4], (ROWS,), 0.5, 3.0, ((0, 32),), jnp.float32)
    member_feats = bell_draw(key_of[5], (ROWS, RE_FEAT), 0.3, 1.8, ((0, 128),), jnp.float32)
    member_ids = draw_member_ids(jax.random.fold_in(key_of[8], 71), 0)
    member_coefs = bell_draw(key_of[7], (MEMBERS, RE_FEAT), 0.25, 1.5, ((0, 128),), jnp.float32)
    return {"feat_values": feat_values, "block_ids": block_ids, "fixed_weights": fixed_weights, "labels": labels, "prior_scores": prior_scores, "member_feats": member_feats, "member_ids": member_ids, "member_coefs": member_coefs}


STEP_SIZE = 0.5
FIXED_RIDGE = 0.1
MEMBER_RIDGE = 1.0
MEMBER_STEP = 0.5
HIGH = lax.Precision.HIGHEST

def reference(feat_values, block_ids, fixed_weights, labels, prior_scores, member_feats, member_ids, member_coefs):
    per_shard = FEAT_BLOCKS // N_FEATURE
    columns = N_FEATURE * KB
    tiles = ROWS // TILE
    tiled = feat_values.reshape(tiles, TILE, columns, BLK)
    owner_base = jnp.arange(columns, dtype=jnp.int32) // KB * per_shard
    global_ids = (block_ids + owner_base[None, :]).astype(jnp.int32)

    def margin_of(weights):
        chosen = weights[global_ids]
        return jnp.einsum('trkb,tkb->tr', tiled, chosen, precision=HIGH).reshape(-1)
    margin = margin_of(fixed_weights)
    probs = jax.nn.sigmoid(margin + prior_scores)
    residual = (probs - labels).reshape(tiles, TILE)
    curvature = (probs * (1.0 - probs)).reshape(tiles, TILE)
    grad_tiles = jnp.einsum('trkb,tr->tkb', tiled, residual, precision=HIGH)
    hess_tiles = jnp.einsum('trkb,tr->tkb', tiled * tiled, curvature, precision=HIGH)
    flat_ids = global_ids.reshape(-1)
    gradient = jax.ops.segment_sum(grad_tiles.reshape(-1, BLK), flat_ids, FEAT_BLOCKS)
    hessian = jax.ops.segment_sum(hess_tiles.reshape(-1, BLK), flat_ids, FEAT_BLOCKS)
    new_weights = fixed_weights - STEP_SIZE * (gradient + FIXED_RIDGE * fixed_weights) / (hessian + 1.0)
    fixed_score = margin_of(new_weights)
    block = math.gcd(ROWS, 4096)
    feats_blocks = member_feats.reshape(-1, block, RE_FEAT)
    ids_blocks = member_ids.reshape(-1, block)
    identity = jnp.eye(RE_FEAT, dtype=jnp.float32)
    coefs = member_coefs
    for sweep in range(NEWTON):
        score = jnp.sum(member_feats * coefs[member_ids], axis=1) + fixed_score
        prob_now = jax.nn.sigmoid(score)
        error = prob_now - labels
        weight = prob_now * (1.0 - prob_now)
        gradient_re = jax.ops.segment_sum(error[:, None] * member_feats, member_ids, MEMBERS) + MEMBER_RIDGE * coefs
        weight_blocks = weight.reshape(-1, block)

        def accumulate(total, pieces):
            feats, wts, ids = pieces
            outer = (wts[:, None] * feats)[:, :, None] * feats[:, None, :]
            return (total + jax.ops.segment_sum(outer, ids, MEMBERS), None)
        start = jnp.zeros((MEMBERS, RE_FEAT, RE_FEAT), jnp.float32)
        hessian_re, unused = lax.scan(accumulate, start, (feats_blocks, weight_blocks, ids_blocks))
        hessian_re = hessian_re + MEMBER_RIDGE * identity[None]
        factor = jnp.linalg.cholesky(hessian_re)
        middle = lax.linalg.triangular_solve(factor, gradient_re[:, :, None], left_side=True, lower=True)
        update = lax.linalg.triangular_solve(factor, middle, left_side=True, lower=True, transpose_a=True)
        coefs = coefs - MEMBER_STEP * update[:, :, 0]
    total = fixed_score + jnp.sum(member_feats * coefs[member_ids], axis=1)
    return (new_weights, coefs, total[:, None])
```

```python
import functools

import jax
import jax.numpy as jnp
from jax import lax
from jax.experimental import pallas as pl
from jax.experimental.pallas import tpu as pltpu
from jax.sharding import PartitionSpec as P

STEP_SIZE = 0.5
FIXED_RIDGE = 0.1
MEMBER_RIDGE = 1.0
MEMBER_STEP = 0.5

F32 = jnp.float32
BF16 = jnp.bfloat16
I32 = jnp.int32

TILES = 16
SLOTS = 4
TILE = 128
BLK = 128
ENTRIES = TILES * SLOTS
PACKET = ENTRIES + 8
DEVICES = 128
SAMPLES = 32
FEATURES = 4
CAP = 8
OWN = 512
POS = DEVICES * CAP
MEM = 32
GROUP = 32

NN = (((1,), (0,)), ((), ()))
NT = (((1,), (1,)), ((), ()))


def split(x, parts):
    out = []
    for _ in range(parts - 1):
        top = x.astype(BF16)
        out.append(top)
        x = x - top.astype(F32)
    out.append(x.astype(BF16))
    return out


def dot(a, b, dims=NN):
    return lax.dot_general(a, b, dims, preferred_element_type=F32)


def dot_right(mask, x, parts, dims=NN):
    return functools.reduce(jnp.add, [dot(mask, piece, dims) for piece in split(x, parts)])


def dot_left(x, mask, parts, dims=NN):
    return functools.reduce(jnp.add, [dot(piece, mask, dims) for piece in split(x, parts)])


def iota(shape, dim):
    return lax.broadcasted_iota(I32, shape, dim)


def onehot(cond):
    return jnp.where(cond, 1.0, 0.0).astype(F32)


def params(mib):
    return pltpu.CompilerParams(vmem_limit_bytes=mib << 20)


def full(shape):
    return pl.BlockSpec(shape, lambda *_: (0,) * len(shape))


def margin_kernel(ids, feats, weights, out, chosen, sems):
    step = pl.program_id(0)

    @pl.when(step == 0)
    def _():
        copies = [
            pltpu.make_async_copy(
                weights.at[pl.ds(ids[j], 1)], chosen.at[pl.ds(j, 1)], sems.at[j]
            )
            for j in range(ENTRIES)
        ]
        for copy in copies:
            copy.start()
        for copy in copies:
            copy.wait()

    tiles = feats.shape[0] // TILE
    rows = []
    for t in range(tiles):
        w = chosen[pl.ds((step * tiles + t) * SLOTS, SLOTS), :]
        total = None
        for k in range(SLOTS):
            term = feats[t * TILE : (t + 1) * TILE, k * BLK : (k + 1) * BLK] * w[k : k + 1, :]
            total = term if total is None else total + term
        rows.append(jnp.sum(total.T, axis=0, keepdims=True))
    out[...] = jnp.concatenate(rows, axis=0)


def first_margin(ids, feats, weights):
    steps = 2
    return pl.pallas_call(
        margin_kernel,
        grid_spec=pltpu.PrefetchScalarGridSpec(
            num_scalar_prefetch=1,
            grid=(steps,),
            in_specs=[
                pl.BlockSpec((TILES * TILE // steps, SLOTS * BLK), lambda i, s: (i, 0)),
                pl.BlockSpec(memory_space=pl.ANY),
            ],
            out_specs=[
                pl.BlockSpec((TILES // steps, TILE), lambda i, s: (i, 0)),
                full((ENTRIES, BLK)),
            ],
            scratch_shapes=[pltpu.SemaphoreType.DMA((ENTRIES,))],
        ),
        out_shape=[
            jax.ShapeDtypeStruct((TILES, TILE), F32),
            jax.ShapeDtypeStruct((ENTRIES, BLK), F32),
        ],
        compiler_params=params(16),
        name="first_margin",
    )(ids, feats, weights)


def stats_kernel(m0, m1, m2, m3, prior, labels, ids, feats, out):
    step = pl.program_id(0)
    tiles = feats.shape[0] // TILE
    at = pl.ds(step * tiles, tiles)
    margin = (m0[at, :] + m1[at, :]) + (m2[at, :] + m3[at, :])
    probs = jax.nn.sigmoid(margin + prior[at, :])
    residual = (probs - labels[at, :]).T
    curvature = (probs * (1.0 - probs)).T
    rows = []
    for t in range(tiles):
        r = jnp.broadcast_to(residual[:, t : t + 1], (TILE, BLK))
        c = jnp.broadcast_to(curvature[:, t : t + 1], (TILE, BLK))
        for k in range(SLOTS):
            x = feats[t * TILE : (t + 1) * TILE, k * BLK : (k + 1) * BLK]
            grad = jnp.sum(x * r, axis=0, keepdims=True)
            hess = jnp.sum(x * x * c, axis=0, keepdims=True)
            rows.append(jnp.concatenate([grad, hess], axis=1))
    out[pl.ds(step * tiles * SLOTS, tiles * SLOTS), :] = jnp.concatenate(rows, axis=0)

    @pl.when(step == 0)
    def _():
        out[ENTRIES:PACKET, :] = ids[...]


def own_stats(margins, prior, labels, ids, feats):
    steps = 2
    small = full((TILES, TILE))
    return pl.pallas_call(
        stats_kernel,
        grid=(steps,),
        in_specs=[small] * 6
        + [
            full((8, 2 * BLK)),
            pl.BlockSpec((TILES * TILE // steps, SLOTS * BLK), lambda i: (i, 0)),
        ],
        out_specs=full((PACKET, 2 * BLK)),
        out_shape=jax.ShapeDtypeStruct((PACKET, 2 * BLK), F32),
        compiler_params=params(16),
        name="own_stats",
    )(*margins, prior, labels, ids, feats)


def second_kernel(packets, own_ids, chosen, feats, place, owners, out):
    lane = iota((1, 128), 1)
    acc = None
    for pair in range(SAMPLES // 2):
        a, b = 2 * pair, 2 * pair + 1
        ids = jnp.where(
            lane < ENTRIES,
            packets[a, ENTRIES : ENTRIES + 1, 0:128],
            packets[b, ENTRIES : ENTRIES + 1, 0:128],
        )
        mask = onehot(own_ids[...] == ids).astype(BF16)
        both = jnp.concatenate([packets[a, 0:ENTRIES, :], packets[b, 0:ENTRIES, :]], axis=0)
        term = dot_right(mask, both, 2)
        acc = term if acc is None else acc + term
    w = chosen[...]
    w = w - STEP_SIZE * (acc[:, :BLK] + FIXED_RIDGE * w) / (acc[:, BLK:] + 1.0)
    ones = jnp.ones((BLK, 128), BF16)
    result = None
    pair = 2 * TILE
    for step in range(TILES // 2):
        parts = []
        for t in (2 * step, 2 * step + 1):
            total = None
            for k in range(SLOTS):
                x = feats[t * TILE : (t + 1) * TILE, k * BLK : (k + 1) * BLK]
                term = x * w[t * SLOTS + k : t * SLOTS + k + 1, :]
                total = term if total is None else total + term
            parts.append(total)
        margin = dot_left(jnp.concatenate(parts, axis=0), ones, 2)
        placed = margin * place[step * pair : (step + 1) * pair, :]
        mask = onehot(
            iota((DEVICES, pair), 0) == owners[0:1, step * pair : (step + 1) * pair]
        ).astype(BF16)
        term = dot_right(mask, placed, 2)
        result = term if result is None else result + term
    out[...] = result


def second_margin(packets, own_ids, chosen, feats, place, owners):
    return pl.pallas_call(
        second_kernel,
        out_shape=jax.ShapeDtypeStruct((DEVICES, 128), F32),
        compiler_params=params(24),
        name="second_margin",
    )(packets, own_ids, chosen, feats, place, owners)


def weights_kernel(ids, order, packets, weights, out, grad, hess):
    step = pl.program_id(0)

    @pl.when(step == 0)
    def _():
        grad[...] = jnp.zeros_like(grad)
        hess[...] = jnp.zeros_like(hess)

        def source(s, carry):
            at = order[s]
            for j in range(ENTRIES):
                row = pl.ds(ids[at * ENTRIES + j], 1)
                grad[row, :] += packets[at, j : j + 1, 0:BLK]
                hess[row, :] += packets[at, j : j + 1, BLK : 2 * BLK]
            return carry

        lax.fori_loop(0, SAMPLES, source, 0)

    rows = weights.shape[0]
    at = pl.ds(step * rows, rows)
    w = weights[...]
    out[...] = w - STEP_SIZE * (grad[at, :] + FIXED_RIDGE * w) / (hess[at, :] + 1.0)


def all_weights(ids, order, packets, weights):
    blocks = weights.shape[0]
    steps = 8
    piece = pl.BlockSpec((blocks // steps, BLK), lambda i, *_: (i, 0))
    return pl.pallas_call(
        weights_kernel,
        grid_spec=pltpu.PrefetchScalarGridSpec(
            num_scalar_prefetch=2,
            grid=(steps,),
            in_specs=[full((SAMPLES, PACKET, 2 * BLK)), piece],
            out_specs=piece,
            scratch_shapes=[pltpu.VMEM((blocks, BLK), F32), pltpu.VMEM((blocks, BLK), F32)],
        ),
        out_shape=jax.ShapeDtypeStruct((blocks, BLK), F32),
        compiler_params=params(24),
        name="all_weights",
    )(ids, order, packets, weights)


def pack_kernel(slots, feats, labels, members, out):
    at = iota((POS, OWN), 0)
    slot = slots[...]
    rows = dot_right(onehot(at == slot).astype(BF16), feats[...], 3)
    out[:, 0:CAP, :] = rows.reshape(DEVICES, CAP, 128)
    owner = slot // CAP
    extra = dot_right(onehot(at == owner * CAP).astype(BF16), labels[...], 3)
    extra += dot_right(onehot(at == owner * CAP + 1).astype(BF16), members[...], 1)
    out[:, CAP : 2 * CAP, :] = extra.reshape(DEVICES, CAP, 128)


def pack_rows(slots, feats, labels, members):
    return pl.pallas_call(
        pack_kernel,
        out_shape=jax.ShapeDtypeStruct((DEVICES, 2 * CAP, 128), F32),
        compiler_params=params(24),
        name="pack_rows",
    )(slots, feats, labels, members)


def spread(block, source):
    group = iota(block.shape, 1) // MEM
    out = None
    for g in range(4):
        shift = (g - source) % 4
        moved = pltpu.roll(block, MEM * shift, 1) if shift else block
        out = moved if out is None else jnp.where(group == g, moved, out)
    return out


def group_kernel(rows, coefs, gram, score, label, live, member, rank, turned, diag):
    lab_parts, mem_parts = [], []
    sub, lane = iota((128, 128), 0), iota((128, 128), 1)
    for b in range(8):
        extra = rows[16 * b : 16 * (b + 1), CAP : 2 * CAP, :].reshape(128, 128)
        first = (lane // CAP) * CAP
        lab_parts.append(jnp.sum(jnp.where(sub == first, extra, 0.0), axis=0, keepdims=True))
        mem_parts.append(jnp.sum(jnp.where(sub == first + 1, extra, 0.0), axis=0, keepdims=True))
    lab = jnp.concatenate(lab_parts, axis=1)
    mem = jnp.concatenate(mem_parts, axis=1).astype(I32) - 1
    member[...] = mem
    few = onehot(iota((MEM, POS), 0) == mem)
    before = onehot(sub < lane).astype(BF16)
    ones = jnp.ones((128, 128), BF16)
    carry = jnp.zeros((MEM, 128), F32)
    ranks = []
    for b in range(8):
        part = few[:, 128 * b : 128 * (b + 1)]
        half = part.astype(BF16)
        count = dot(half, before) + carry
        carry = carry + dot(half, ones)
        ranks.append(jnp.sum(part * count, axis=0, keepdims=True))
    rnk = jnp.concatenate(ranks, axis=1).astype(I32)
    rank[...] = rnk
    by_rank = onehot((iota((GROUP, POS), 0) == rnk) & (mem >= 0))
    by_member = onehot((iota((128, POS), 0) % MEM) == mem).astype(BF16)
    label[...] = dot_left(by_rank * lab, by_member, 3, NT)
    live[...] = dot(by_rank.astype(BF16), by_member, NT)
    target = jnp.where(mem >= 0, rnk * MEM + mem, -1)
    feats = rows[:, 0:CAP, :].reshape(POS, 128).T
    pieces = split(feats, 3)
    for b in range(4):
        goal = onehot(iota((256, POS), 0) + 256 * b == target).astype(BF16)
        moved = dot(pieces[0], goal, NT) + dot(pieces[1], goal, NT) + dot(pieces[2], goal, NT)
        turned[0, :, 256 * b : 256 * (b + 1)] = moved
    x = turned[0]
    for p in range(1, 4):
        turned[p] = pltpu.roll(x, POS - MEM * p, 1)
    c = coefs[...].T
    own = jnp.sum(x * jnp.concatenate([c] * 8, axis=1), axis=0, keepdims=True)
    own = jnp.where(iota((GROUP, POS), 1) // MEM == iota((GROUP, POS), 0), own, 0.0)
    folded = own[:, 0:128]
    for b in range(1, 8):
        folded = folded + own[:, 128 * b : 128 * (b + 1)]
    folded = folded + pltpu.roll(folded, 64, 1)
    score[...] = folded + pltpu.roll(folded, 32, 1)
    for delta in range(GROUP // 2 + 1):
        p, q = delta % 4, delta // 4
        for b in range(8):
            o = (b + q) % 8
            prod = turned[0, :, 128 * b : 128 * (b + 1)] * turned[p, :, 128 * o : 128 * (o + 1)]
            diag[delta : delta + 1, 128 * b : 128 * (b + 1)] = jnp.sum(prod, axis=0, keepdims=True)
    for delta in range(GROUP // 2 + 1, GROUP):
        diag[delta : delta + 1, :] = pltpu.roll(
            jnp.broadcast_to(diag[GROUP - delta : GROUP - delta + 1, :], (8, POS)), POS - MEM * delta, 1
        )[0:1, :]
    for b in range(8):
        block = diag[:, 128 * b : 128 * (b + 1)]
        for p in range(4):
            i = 4 * b + p
            wide = spread(block, p)
            gram[i] = pltpu.roll(wide, i, 0) if i else wide


def group_rows(rows, coefs):
    small = jax.ShapeDtypeStruct((GROUP, 128), F32)
    line = jax.ShapeDtypeStruct((1, POS), I32)
    return pl.pallas_call(
        group_kernel,
        out_shape=[
            jax.ShapeDtypeStruct((GROUP, GROUP, 128), F32),
            small,
            small,
            small,
            line,
            line,
        ],
        scratch_shapes=[pltpu.VMEM((4, 128, POS), F32), pltpu.VMEM((GROUP, POS), F32)],
        compiler_params=params(32),
        name="group_rows",
    )(rows, coefs)


def gram_times(gram, v):
    out = None
    for i in range(GROUP):
        term = gram[i] * v[i : i + 1, :]
        out = term if out is None else out + term
    return out


def solve_kernel(parts, gram, score, label, live, member, rank, back, steps, work):
    sub, lane = iota((128, 128), 0), iota((128, 128), 1)
    got = parts[...]
    fixed = []
    for b in range(8):
        keep = sub // FEATURES == 4 * b + lane // 32
        fixed.append(jnp.sum(jnp.where(keep, got, 0.0), axis=0, keepdims=True))
    fixed = jnp.concatenate(fixed, axis=1)
    mem = member[...]
    by_rank = onehot((iota((GROUP, POS), 0) == rank[...]) & (mem >= 0))
    by_member = onehot((iota((128, POS), 0) % MEM) == mem).astype(BF16)
    offset = dot_left(by_rank * fixed, by_member, 2, NT)
    alive = live[...]
    y = label[...]
    s = score[...]
    at = iota((GROUP, 128), 0)
    steps_total = None
    for sweep in range(2):
        p = jax.nn.sigmoid(s + offset)
        error = (p - y) * alive
        d = jnp.sqrt(p * (1.0 - p) * alive)
        b = d * (gram_times(gram, error) + s)
        for i in range(GROUP):
            row = gram[i] * (d * d[i : i + 1, :])
            work[i] = row + onehot(at == i)
        for k in range(GROUP):
            row = work[k]
            inverse = 1.0 / row[k : k + 1, :]
            scaled = jnp.where(at == k, 1.0 - inverse, row * inverse)
            b = b - b[k : k + 1, :] * scaled
            for i in range(k + 1, GROUP):
                work[i] = work[i] - row[i : i + 1, :] * scaled
        u = error - d * b
        s = s - MEMBER_STEP * (gram_times(gram, u) + MEMBER_RIDGE * s)
        steps_total = u * 0.25 if sweep == 0 else steps_total + u * 0.5
    steps[...] = steps_total
    final = (s + offset) * 0.25
    scores = jnp.sum(by_rank * dot_left(final, by_member, 2), axis=0, keepdims=True)
    for b in range(8):
        line = jnp.broadcast_to(scores[:, 128 * b : 128 * (b + 1)], (16, 128))
        back[16 * b : 16 * (b + 1), :] = jnp.where(
            iota((16, 128), 1) // CAP == iota((16, 128), 0), line, 0.0
        )


def solve_members(parts, gram, score, label, live, member, rank):
    return pl.pallas_call(
        solve_kernel,
        out_shape=[
            jax.ShapeDtypeStruct((DEVICES, 128), F32),
            jax.ShapeDtypeStruct((GROUP, 128), F32),
        ],
        scratch_shapes=[pltpu.VMEM((GROUP, GROUP, 128), F32)],
        compiler_params=params(16),
        name="solve_members",
    )(parts, gram, score, label, live, member, rank)


def coefs_kernel(rows, coefs, steps, member, rank, out):
    mem = member[...]
    by_rank = onehot((iota((GROUP, POS), 0) == rank[...]) & (mem >= 0))
    by_member = onehot((iota((128, POS), 0) % MEM) == mem)
    line = jnp.sum(
        by_rank * dot_left(steps[...] * 0.25, by_member.astype(BF16), 2), axis=0, keepdims=True
    )
    weighted = split(by_member[0:MEM, :] * line, 2)
    feats = split(rows[:, 0:CAP, :].reshape(POS, 128), 2)
    moved = dot(weighted[0], feats[0]) + dot(weighted[0], feats[1]) + dot(weighted[1], feats[0])
    out[...] = 0.25 * coefs[...] - moved


def new_coefs(rows, coefs, steps, member, rank):
    return pl.pallas_call(
        coefs_kernel,
        out_shape=jax.ShapeDtypeStruct((MEM, 128), F32),
        compiler_params=params(16),
        name="new_coefs",
    )(rows, coefs, steps, member, rank)


def total_kernel(back, slots, out):
    slot = slots[...]
    mask = onehot(iota((DEVICES, OWN), 0) == slot // CAP).astype(BF16)
    moved = dot_left(back[...].T, mask, 2)
    keep = (iota((128, OWN), 0) % CAP) == slot % CAP
    out[...] = jnp.sum(jnp.where(keep, moved, 0.0), axis=0, keepdims=True)


def total_rows(back, slots):
    return pl.pallas_call(
        total_kernel,
        out_shape=jax.ShapeDtypeStruct((1, OWN), F32),
        compiler_params=params(16),
        name="total_rows",
    )(back, slots)


def ring_feature(value):
    pairs = [[(i, (i + k) % FEATURES) for i in range(FEATURES)] for k in range(FEATURES)]
    return [value] + [lax.ppermute(value, "feature", pairs[k]) for k in (1, 3, 2)]


def sample_pairs(shift, first):
    pairs = []
    for i in range(SAMPLES):
        x, z, core = i // 8, (i // 2) % 4, i % 2
        if (core == 0) == first:
            z = (z + shift) % 4
        else:
            x = (x + shift) % 4
        pairs.append((i, (x * 4 + z) * 2 + core))
    return pairs


def gather_sample(value):
    for first in (True, False):
        value = jnp.concatenate(
            [value]
            + [lax.ppermute(value, "sample", sample_pairs(k, first)) for k in (1, 2, 3)],
            axis=0,
        )
    other = lax.ppermute(value, "sample", [(i, i ^ 1) for i in range(SAMPLES)])
    return jnp.concatenate([value, other], axis=0)


def gathered_order():
    me = lax.axis_index("sample")
    x, z, core = me // 8, (me // 2) % 4, me % 2
    source = jnp.arange(SAMPLES, dtype=I32)
    xs, zs, cs = source // 8, (source // 2) % 4, source % 2
    along_x, along_z = (x - xs) % 4, (z - zs) % 4
    late = jnp.where(cs == 0, along_x, along_z)
    early = jnp.where(cs == 0, along_z, along_x)
    return (jnp.where(cs == core, 0, 16) + late * 4 + early).astype(I32)


def exchange(value):
    return lax.all_to_all(value, ("sample", "feature"), split_axis=0, concat_axis=0, tiled=True)


def shards(
    feat_values,
    block_ids,
    fixed_weights,
    labels,
    prior_scores,
    member_feats,
    member_ids,
    member_coefs,
):
    flat_ids = block_ids.reshape(-1)
    float_ids = flat_ids.astype(F32)
    feature = lax.axis_index("feature")

    owner = member_ids // MEM
    span = jnp.arange(OWN, dtype=I32)
    earlier = (owner[None, :] == owner[:, None]) & (span[None, :] < span[:, None])
    rank = jnp.sum(earlier.astype(I32), axis=1)
    slots = owner * CAP + rank

    margin, chosen = first_margin(flat_ids, feat_values, fixed_weights)
    margins = ring_feature(margin)

    ring = ring_feature(slots)
    shift = (0, 1, 3, 2)
    quarter = jnp.arange(FEATURES, dtype=I32)
    every = functools.reduce(
        jnp.add,
        [
            jnp.where((quarter == (feature - k) % FEATURES)[:, None], r[None, :], 0)
            for k, r in zip(shift, ring)
        ],
    )
    lanes = jnp.arange(128, dtype=I32)
    column = (quarter[:, None] * CAP + every % CAP).reshape(-1)
    place = (lanes[None, :] % 32 == column[:, None]).astype(F32)
    owners = (every // CAP).reshape(1, -1)

    id_rows = jnp.tile(float_ids[None, :], (8, 4))
    packet = own_stats(
        margins, prior_scores.reshape(TILES, TILE), labels.reshape(TILES, TILE), id_rows, feat_values
    )

    own_labels = lax.dynamic_slice_in_dim(labels, feature * OWN, OWN, 0)
    mine = lanes[None, :] % CAP == rank[:, None]
    label_rows = jnp.where(mine, own_labels[:, None], 0.0)
    member_rows = jnp.where(mine, (member_ids % MEM + 1).astype(F32)[:, None], 0.0)
    packed = pack_rows(slots[None, :], member_feats, label_rows, member_rows)
    packed, packet = lax.optimization_barrier((packed, packet))
    rows = exchange(packed)
    packets = gather_sample(packet[None])

    gram, score, label, live, member, rank_in = group_rows(rows, jnp.tile(member_coefs, (4, 1)))

    own_ids = jnp.broadcast_to(float_ids[:, None], (ENTRIES, 128))
    partial = second_margin(packets, own_ids, chosen, feat_values, place, owners)
    parts = exchange(partial[:, None, :])[:, 0, :]

    all_ids = packets[:, ENTRIES, :ENTRIES].astype(I32).reshape(-1)
    weights = all_weights(all_ids, gathered_order(), packets, fixed_weights)

    back, steps = solve_members(parts, gram, score, label, live, member, rank_in)
    returned = exchange(back[:, None, :])[:, 0, :]
    coefs = new_coefs(rows, member_coefs, steps, member, rank_in)
    total = total_rows(returned, slots[None, :])
    return (weights, coefs, total.reshape(OWN, 1))


def solution(mesh):
    both = ("sample", "feature")
    in_specs = (
        P("sample", "feature"),
        P("sample", "feature"),
        P("feature", None),
        P("sample"),
        P("sample"),
        P(both, None),
        P(both),
        P(both, None),
    )
    out_specs = (P("feature", None), P(both, None), P(both, None))
    return jax.shard_map(shards, mesh=mesh, in_specs=in_specs, out_specs=out_specs, check_vma=False)
```

```python
import functools

import jax
import jax.numpy as jnp
from jax import lax
from jax.experimental import pallas as pl
from jax.experimental.pallas import tpu as pltpu
from jax.sharding import PartitionSpec as P

STEP_SIZE = 0.5
FIXED_RIDGE = 0.1
MEMBER_RIDGE = 1.0
MEMBER_STEP = 0.5

F32 = jnp.float32
BF16 = jnp.bfloat16
I32 = jnp.int32

TILES = 16
SLOTS = 4
TILE = 128
BLK = 128
ENTRIES = TILES * SLOTS
PACKET = ENTRIES + 8
DEVICES = 128
SAMPLES = 32
FEATURES = 4
CAP = 8
OWN = 512
POS = DEVICES * CAP
NOTE = CAP + 1
MEM = 32
GROUP = 32
RING = (0, 1, 3, 2)

NN = (((1,), (0,)), ((), ()))
NT = (((1,), (1,)), ((), ()))


def split(x, parts):
    out = []
    for _ in range(parts - 1):
        top = x.astype(BF16)
        out.append(top)
        x = x - top.astype(F32)
    out.append(x.astype(BF16))
    return out


def dot(a, b, dims=NN):
    return lax.dot_general(a, b, dims, preferred_element_type=F32)


def dot_right(mask, x, parts, dims=NN):
    return functools.reduce(jnp.add, [dot(mask, piece, dims) for piece in split(x, parts)])


def dot_left(x, mask, parts, dims=NN):
    return functools.reduce(jnp.add, [dot(piece, mask, dims) for piece in split(x, parts)])


def iota(shape, dim):
    return lax.broadcasted_iota(I32, shape, dim)


def onehot(cond):
    return jnp.where(cond, 1.0, 0.0).astype(F32)


def params(mib):
    return pltpu.CompilerParams(vmem_limit_bytes=mib << 20)


HBM = pl.BlockSpec(memory_space=pltpu.HBM)
ANY = pl.BlockSpec(memory_space=pl.ANY)
VMEM = pl.BlockSpec(memory_space=pltpu.VMEM)
SMEM = pl.BlockSpec(memory_space=pltpu.SMEM)
CHUNKS = 8
WIDE = 50


def fetch(source, target, sems, chunks=CHUNKS):
    rows = source.shape[0] // chunks
    copies = [
        pltpu.make_async_copy(
            source.at[pl.ds(i * rows, rows)], target.at[pl.ds(i * rows, rows)], sems.at[i]
        )
        for i in range(chunks)
    ]
    for copy in copies:
        copy.start()
    return copies


def tile_margin(feats, weights, t):
    total = None
    for k in range(SLOTS):
        x = feats[t * TILE : (t + 1) * TILE, k * BLK : (k + 1) * BLK]
        e = t * SLOTS + k
        term = x * weights[e : e + 1, :]
        total = term if total is None else total + term
    return total


def margin_kernel(
    ids, members, feats, weights, out, chosen, own, sent, merge, held, row_sems, sems
):
    copies = fetch(feats, held, sems)
    picked = [
        pltpu.make_async_copy(
            weights.at[pl.ds(ids[e % SLOTS, e // SLOTS], 1)], chosen.at[pl.ds(e, 1)], row_sems.at[e]
        )
        for e in range(ENTRIES)
    ]
    for copy in picked:
        copy.start()

    owner = members[...] // MEM
    column = owner.astype(F32).T.astype(I32)
    sub, lane = iota((TILE, TILE), 0), iota((TILE, TILE), 1)
    for a in range(4):
        rank = None
        for b in range(a + 1):
            same = jnp.broadcast_to(column[:, b : b + 1], (TILE, TILE)) == owner[a : a + 1, :]
            if a == b:
                same = same & (sub < lane)
            term = jnp.sum(onehot(same), axis=0, keepdims=True)
            rank = term if rank is None else rank + term
        out[TILES + a : TILES + a + 1, :] = owner[a : a + 1, :].astype(F32) * CAP + rank
    out[TILES + 4 :, :] = jnp.zeros((4, TILE), F32)

    at, of = iota((ENTRIES, 128), 0), iota((ENTRIES, 128), 1) % ENTRIES
    rows = jnp.zeros((ENTRIES, 128), I32)
    line = jnp.zeros((8, 128), I32)
    for e in range(ENTRIES):
        block = ids[e % SLOTS, e // SLOTS]
        rows = jnp.where(at == e, block, rows)
        line = jnp.where(of[0:8, :] == e, block, line)
    same = rows == line[0:1, :]
    repeat = jnp.sum(onehot(same & (at < of)), axis=0, keepdims=True)
    own[...] = rows.astype(F32)
    kept = jnp.where(repeat > 0.0, weights.shape[0], line[0:1, :]).astype(F32)
    sent[...] = jnp.broadcast_to(jnp.concatenate([kept, kept], axis=1), (8, 256))
    earlier = jnp.sum(onehot(same & (of < at)), axis=1, keepdims=True)
    merge[...] = jnp.where(earlier > 0.0, 0.0, onehot(same))

    for copy in picked:
        copy.wait()
    each = TILES // CHUNKS
    for c in range(CHUNKS):
        copies[c].wait()
        for t in range(c * each, (c + 1) * each):
            out[t : t + 1, :] = jnp.sum(tile_margin(held, chosen, t).T, axis=0, keepdims=True)


def first_margin(ids, members, feats, weights):
    table = jax.ShapeDtypeStruct((ENTRIES, BLK), F32)
    return pl.pallas_call(
        margin_kernel,
        in_specs=[SMEM, VMEM, HBM, HBM],
        out_shape=[
            jax.ShapeDtypeStruct((TILES + 8, TILE), F32),
            table,
            table,
            jax.ShapeDtypeStruct((8, 2 * BLK), F32),
            table,
        ],
        scratch_shapes=[
            pltpu.VMEM((TILES * TILE, SLOTS * BLK), F32),
            pltpu.SemaphoreType.DMA((ENTRIES,)),
            pltpu.SemaphoreType.DMA((CHUNKS,)),
        ],
        compiler_params=params(WIDE),
        name="first_margin",
    )(ids, members, feats, weights)


def stats_kernel(m0, m1, m2, m3, prior, labels, ids, merge, feats, out, held, raw, sems):
    copies = fetch(feats, held, sems)
    margin = (m0[0:TILES, :] + m1[0:TILES, :]) + (m2[0:TILES, :] + m3[0:TILES, :])
    probs = jax.nn.sigmoid(margin + prior[...])
    residual = (probs - labels[...]).T
    curvature = (probs * (1.0 - probs)).T
    each = TILES // CHUNKS
    for t in range(TILES):
        if t % each == 0:
            copies[t // each].wait()
        r = jnp.broadcast_to(residual[:, t : t + 1], (TILE, BLK))
        c = jnp.broadcast_to(curvature[:, t : t + 1], (TILE, BLK))
        for k in range(SLOTS):
            x = held[t * TILE : (t + 1) * TILE, k * BLK : (k + 1) * BLK]
            e = t * SLOTS + k
            raw[e : e + 1, 0:BLK] = jnp.sum(x * r, axis=0, keepdims=True)
            raw[e : e + 1, BLK : 2 * BLK] = jnp.sum(x * x * c, axis=0, keepdims=True)
    out[0:ENTRIES, :] = dot_right(merge[:, 0:ENTRIES].astype(BF16), raw[...], 3)
    out[ENTRIES:PACKET, :] = ids[...]


def own_stats(margins, prior, labels, ids, merge, feats):
    return pl.pallas_call(
        stats_kernel,
        in_specs=[VMEM] * 8 + [HBM],
        out_shape=jax.ShapeDtypeStruct((PACKET, 2 * BLK), F32),
        scratch_shapes=[
            pltpu.VMEM((TILES * TILE, SLOTS * BLK), F32),
            pltpu.VMEM((ENTRIES, 2 * BLK), F32),
            pltpu.SemaphoreType.DMA((CHUNKS,)),
        ],
        compiler_params=params(WIDE),
        name="own_stats",
    )(*margins, prior, labels, ids, merge, feats)


def second_kernel(own_ids, chosen, packed, feats, *rest):
    margins, pieces, (out, held, sent, slots, sems, piece_sems) = rest[:4], rest[4:12], rest[12:]
    arrivals = [
        pltpu.make_async_copy(piece, sent.at[pl.ds(4 * PACKET * i, 4 * PACKET)], piece_sems.at[i])
        for i, piece in enumerate(pieces)
    ]
    for copy in arrivals:
        copy.start()
    copies = fetch(feats, held, sems)
    lane = iota((1, 128), 1)
    acc = None
    for pair in range(SAMPLES // 2):
        a, b = 2 * pair, 2 * pair + 1
        if a % 4 == 0:
            arrivals[a // 4].wait()
        a, b = a * PACKET, b * PACKET
        ids = jnp.where(
            lane < ENTRIES,
            sent[a + ENTRIES : a + ENTRIES + 1, 0:128],
            sent[b + ENTRIES : b + ENTRIES + 1, 0:128],
        )
        mask = onehot(own_ids[...] == ids).astype(BF16)
        both = jnp.concatenate([sent[a : a + ENTRIES, :], sent[b : b + ENTRIES, :]], axis=0)
        term = dot_right(mask, both, 2)
        acc = term if acc is None else acc + term
    w = chosen[...]
    w = w - STEP_SIZE * (acc[:, :BLK] + FIXED_RIDGE * w) / (acc[:, BLK:] + 1.0)
    ones = jnp.ones((BLK, 128), BF16)
    feature = lax.axis_index("feature")
    for shift, margin in zip(RING, margins):
        source = lax.rem(feature + FEATURES - shift, FEATURES)
        slots[pl.ds(source * 4, 4), :] = margin[TILES : TILES + 4, :]
    slot = slots[...].astype(I32)
    column = (slot % CAP + CAP * (iota((TILES, TILE), 0) // 4)).astype(F32).T
    owner = slot // CAP
    result = None
    lanes = (iota((TILE, 128), 1) % 32).astype(F32)
    for t in range(0, TILES, 2):
        copies[t // 2].wait()
        both = [tile_margin(held, w, t), tile_margin(held, w, t + 1)]
        margin = dot_left(jnp.concatenate(both, axis=0), ones, 2)
        place = [
            lanes == jnp.broadcast_to(column[:, q : q + 1], (TILE, 128)) for q in (t, t + 1)
        ]
        placed = jnp.where(jnp.concatenate(place, axis=0), margin, 0.0)
        owners = jnp.concatenate([owner[t : t + 1, :], owner[t + 1 : t + 2, :]], axis=1)
        mask = onehot(iota((DEVICES, 2 * TILE), 0) == owners).astype(BF16)
        term = dot_right(mask, placed, 2)
        result = term if result is None else result + term
    out[...] = packed[...]
    result = jnp.where(iota((DEVICES, 128), 1) < 32, result, 0.0)
    for d in range(DEVICES):
        at = NOTE * d + CAP
        out[at : at + 1, :] = packed[at : at + 1, :] + result[d : d + 1, :]


def second_margin(pieces, own_ids, chosen, margins, packed, feats):
    return pl.pallas_call(
        second_kernel,
        in_specs=[VMEM] * 3 + [HBM] + [VMEM] * 4 + [ANY] * 8,
        out_shape=jax.ShapeDtypeStruct((DEVICES * NOTE, 128), F32),
        scratch_shapes=[
            pltpu.VMEM((TILES * TILE, SLOTS * BLK), F32),
            pltpu.VMEM((SAMPLES * PACKET, 2 * BLK), F32),
            pltpu.VMEM((TILES, TILE), F32),
            pltpu.SemaphoreType.DMA((CHUNKS,)),
            pltpu.SemaphoreType.DMA((8,)),
        ],
        compiler_params=params(WIDE),
        name="second_margin",
    )(own_ids, chosen, packed, feats, *margins, *pieces)


def gathered_place(source):
    me = lax.axis_index("sample")
    x, z, core = me // 8, (me // 2) % 4, me % 2
    xs, zs, cs = source // 8, (source // 2) % 4, source % 2
    along_x, along_z = (x - xs + 4) % 4, (z - zs + 4) % 4
    late = jnp.where(cs == 0, along_x, along_z)
    early = jnp.where(cs == 0, along_z, along_x)
    return jnp.where(cs == core, 0, 16) + late * 4 + early


def weights_kernel(weights, *rest):
    pieces, rest = rest[:8], rest[8:]
    out, held, grad, hess, sent, table, ids, in_sems, out_sems, piece_sems, id_sem = rest
    blocks = weights.shape[0]
    arrivals = [
        pltpu.make_async_copy(piece, sent.at[pl.ds(4 * PACKET * i, 4 * PACKET)], piece_sems.at[i])
        for i, piece in enumerate(pieces)
    ]
    for copy in arrivals:
        copy.start()
    copies = fetch(weights, held, in_sems)

    def clear(i, carry):
        at = pl.ds(pl.multiple_of(i * 256, 256), 256)
        grad[at, :] = jnp.zeros((256, BLK), F32)
        hess[at, :] = jnp.zeros((256, BLK), F32)
        return carry

    lax.fori_loop(0, blocks // 256, clear, 0)
    for copy in arrivals:
        copy.wait()

    lines = [sent[i * PACKET + ENTRIES : i * PACKET + ENTRIES + 1, 0:128] for i in range(SAMPLES)]
    table[...] = jnp.concatenate(lines, axis=0).astype(I32)
    copy = pltpu.make_async_copy(table, ids, id_sem)
    copy.start()
    copy.wait()

    def source(s, carry):
        at = gathered_place(s)
        packet = sent.at[pl.ds(pl.multiple_of(at * PACKET, 8), PACKET)]
        for first in range(0, ENTRIES, 16):
            span = range(first, first + 16)
            rows = [pl.ds(ids[at, j], 1) for j in span]
            old = [(grad[r, :], hess[r, :]) for r in rows]
            new = [
                (g + packet[j : j + 1, 0:BLK], h + packet[j : j + 1, BLK : 2 * BLK])
                for j, (g, h) in zip(span, old)
            ]
            for r, (g, h) in zip(rows, new):
                grad[r, :] = g
                hess[r, :] = h
        return carry

    lax.fori_loop(0, SAMPLES, source, 0)
    size = blocks // CHUNKS
    done = []
    for c in range(CHUNKS):
        copies[c].wait()

        def update(i, carry, c=c):
            at = pl.ds(pl.multiple_of(c * size + i * 256, 256), 256)
            w = held[at, :]
            held[at, :] = w - STEP_SIZE * (grad[at, :] + FIXED_RIDGE * w) / (hess[at, :] + 1.0)
            return carry

        lax.fori_loop(0, size // 256, update, 0)
        at = pl.ds(c * size, size)
        copy = pltpu.make_async_copy(held.at[at], out.at[at], out_sems.at[c])
        copy.start()
        done.append(copy)
    for copy in done:
        copy.wait()


def all_weights(pieces, weights):
    blocks = weights.shape[0]
    return pl.pallas_call(
        weights_kernel,
        in_specs=[HBM] + [ANY] * 8,
        out_specs=HBM,
        out_shape=jax.ShapeDtypeStruct((blocks, BLK), F32),
        scratch_shapes=[
            pltpu.VMEM((blocks, BLK), F32),
            pltpu.VMEM((blocks + 8, BLK), F32),
            pltpu.VMEM((blocks + 8, BLK), F32),
            pltpu.VMEM((SAMPLES * PACKET, 2 * BLK), F32),
            pltpu.VMEM((SAMPLES, 128), I32),
            pltpu.SMEM((SAMPLES, 128), I32),
            pltpu.SemaphoreType.DMA((CHUNKS,)),
            pltpu.SemaphoreType.DMA((CHUNKS,)),
            pltpu.SemaphoreType.DMA((8,)),
            pltpu.SemaphoreType.DMA,
        ],
        compiler_params=params(WIDE),
        name="all_weights",
    )(weights, *pieces)


def pack_kernel(margin, members, labels, feats, out, slot, placed):
    feature = lax.axis_index("feature")
    slots = margin[TILES : TILES + 4, :].astype(I32)
    own = labels[pl.ds(feature * 4, 4), :]
    local = (members[...] % MEM + 1).astype(F32)
    columns = jnp.concatenate([(slots % CAP).astype(F32), own, local], axis=0).T
    lane = iota((TILE, 128), 1)
    within = (lane % CAP).astype(F32)
    for a in range(4):
        slot[:, a * TILE : (a + 1) * TILE] = slots[a : a + 1, :]
        rank, label, member = (
            jnp.broadcast_to(columns[:, 4 * q + a : 4 * q + a + 1], (TILE, 128)) for q in range(3)
        )
        value = jnp.where(lane // CAP == 4, label, jnp.where(lane // CAP == 5, member, 0.0))
        placed[a * TILE : (a + 1) * TILE, :] = jnp.where(within == rank, value, 0.0)
    line = slot[...]
    rows = dot_right(onehot(iota((POS, OWN), 0) == line).astype(BF16), feats[...], 3)
    notes = dot_right(onehot(iota((DEVICES, OWN), 0) == line // CAP).astype(BF16), placed[...], 3)
    for d in range(DEVICES):
        out[NOTE * d : NOTE * d + CAP, :] = rows[CAP * d : CAP * (d + 1), :]
        out[NOTE * d + CAP : NOTE * (d + 1), :] = notes[d : d + 1, :]


def pack_rows(margin, members, labels, feats):
    return pl.pallas_call(
        pack_kernel,
        out_shape=[
            jax.ShapeDtypeStruct((DEVICES * NOTE, 128), F32),
            jax.ShapeDtypeStruct((1, OWN), I32),
        ],
        scratch_shapes=[pltpu.VMEM((OWN, 128), F32)],
        compiler_params=params(WIDE),
        name="pack_rows",
    )(margin, members, labels, feats)


def gram_times(gram, v):
    out = None
    for i in range(GROUP):
        term = gram[i] * v[i : i + 1, :]
        out = term if out is None else out + term
    return out


def spread(block, source):
    group = iota(block.shape, 1) // MEM
    out = None
    for g in range(4):
        shift = (g - source) % 4
        moved = pltpu.roll(block, MEM * shift, 1) if shift else block
        out = moved if out is None else jnp.where(group == g, moved, out)
    return out


def unpack(rows, feats, notes=None):
    for d in range(DEVICES):
        feats[CAP * d : CAP * (d + 1), :] = rows[NOTE * d : NOTE * d + CAP, :]
        if notes is not None:
            notes[d : d + 1, :] = rows[NOTE * d + CAP : NOTE * (d + 1), :]


def repeat_lanes(x, first, size):
    lane = iota(x.shape, 1)
    x = jnp.where((lane >= first) & (lane < first + size), x, 0.0)
    while size < 128:
        x = x + pltpu.roll(x, size, 1)
        size *= 2
    return x


def owner_kernel(rows, coefs, back, steps, lines, turned, diag, gram, work, held, notes):
    unpack(rows, held, notes)
    sub, lane = iota((128, 128), 0), iota((128, 128), 1)
    lab_parts, mem_parts, fixed_parts = [], [], []
    labs = repeat_lanes(notes[...], 4 * CAP, CAP)
    mems = repeat_lanes(notes[...], 5 * CAP, CAP)
    got = repeat_lanes(notes[...], 0, 32)
    for b in range(8):
        at = slice(16 * b, 16 * (b + 1))
        keep = iota((16, 128), 0) == iota((16, 128), 1) // CAP
        lab_parts.append(jnp.sum(jnp.where(keep, labs[at, :], 0.0), axis=0, keepdims=True))
        mem_parts.append(jnp.sum(jnp.where(keep, mems[at, :], 0.0), axis=0, keepdims=True))
        keep = iota((16, 128), 0) // FEATURES == iota((16, 128), 1) // 32
        fixed_parts.append(jnp.sum(jnp.where(keep, got[at, :], 0.0), axis=0, keepdims=True))
    lab = jnp.concatenate(lab_parts, axis=1)
    fixed = jnp.concatenate(fixed_parts, axis=1)
    mem = jnp.concatenate(mem_parts, axis=1).astype(I32) - 1
    few = onehot(iota((MEM, POS), 0) == mem)
    before = onehot(sub < lane).astype(BF16)
    ones = jnp.ones((128, 128), BF16)
    carry = jnp.zeros((MEM, 128), F32)
    ranks = []
    for b in range(8):
        part = few[:, 128 * b : 128 * (b + 1)]
        half = part.astype(BF16)
        count = dot(half, before) + carry
        carry = carry + dot(half, ones)
        ranks.append(jnp.sum(part * count, axis=0, keepdims=True))
    rnk = jnp.concatenate(ranks, axis=1).astype(I32)
    lines[0:8, :] = jnp.broadcast_to(mem, (8, POS))
    lines[8:16, :] = jnp.broadcast_to(rnk, (8, POS))
    by_rank = onehot((iota((GROUP, POS), 0) == rnk) & (mem >= 0))
    by_member = onehot((iota((128, POS), 0) % MEM) == mem).astype(BF16)
    y = dot_left(by_rank * lab, by_member, 3, NT)
    offset = dot_left(by_rank * fixed, by_member, 2, NT)
    alive = dot(by_rank.astype(BF16), by_member, NT)
    target = jnp.where(mem >= 0, rnk * MEM + mem, -1)
    feats = held[...].T
    pieces = split(feats, 3)
    for b in range(4):
        goal = onehot(iota((256, POS), 0) + 256 * b == target).astype(BF16)
        moved = dot(pieces[0], goal, NT) + dot(pieces[1], goal, NT) + dot(pieces[2], goal, NT)
        turned[0, :, 256 * b : 256 * (b + 1)] = moved
    x = turned[0]
    for p in range(1, 4):
        turned[p] = pltpu.roll(x, POS - MEM * p, 1)
    c = jnp.concatenate([coefs[...]] * 4, axis=0).T
    own = jnp.sum(x * jnp.concatenate([c] * 8, axis=1), axis=0, keepdims=True)
    own = jnp.where(iota((GROUP, POS), 1) // MEM == iota((GROUP, POS), 0), own, 0.0)
    folded = own[:, 0:128]
    for b in range(1, 8):
        folded = folded + own[:, 128 * b : 128 * (b + 1)]
    folded = folded + pltpu.roll(folded, 64, 1)
    s = folded + pltpu.roll(folded, 32, 1)
    for delta in range(GROUP // 2 + 1):
        p, q = delta % 4, delta // 4
        for b in range(8):
            o = (b + q) % 8
            prod = turned[0, :, 128 * b : 128 * (b + 1)] * turned[p, :, 128 * o : 128 * (o + 1)]
            diag[delta : delta + 1, 128 * b : 128 * (b + 1)] = jnp.sum(prod, axis=0, keepdims=True)
    for delta in range(GROUP // 2 + 1, GROUP):
        diag[delta : delta + 1, :] = pltpu.roll(
            jnp.broadcast_to(diag[GROUP - delta : GROUP - delta + 1, :], (8, POS)), POS - MEM * delta, 1
        )[0:1, :]
    for b in range(8):
        block = diag[:, 128 * b : 128 * (b + 1)]
        for p in range(4):
            i = 4 * b + p
            wide = spread(block, p)
            gram[i] = pltpu.roll(wide, i, 0) if i else wide
    at = iota((GROUP, 128), 0)
    steps_total = None
    for sweep in range(2):
        p = jax.nn.sigmoid(s + offset)
        error = (p - y) * alive
        d = jnp.sqrt(p * (1.0 - p) * alive)
        b = d * (gram_times(gram, error) + s)
        for i in range(GROUP):
            row = gram[i] * (d * d[i : i + 1, :])
            work[i] = row + onehot(at == i)
        for k in range(GROUP):
            row = work[k]
            inverse = 1.0 / row[k : k + 1, :]
            scaled = jnp.where(at == k, 1.0 - inverse, row * inverse)
            b = b - b[k : k + 1, :] * scaled
            for i in range(k + 1, GROUP):
                work[i] = work[i] - row[i : i + 1, :] * scaled
        u = error - d * b
        s = s - MEMBER_STEP * (gram_times(gram, u) + MEMBER_RIDGE * s)
        steps_total = u * 0.25 if sweep == 0 else steps_total + u * 0.5
    steps[...] = steps_total
    final = (s + offset) * 0.25
    scores = jnp.sum(by_rank * dot_left(final, by_member, 2), axis=0, keepdims=True)
    for b in range(8):
        line = jnp.broadcast_to(scores[:, 128 * b : 128 * (b + 1)], (16, 128))
        back[16 * b : 16 * (b + 1), :] = jnp.where(
            iota((16, 128), 1) // CAP == iota((16, 128), 0), line, 0.0
        )


def owner_work(rows, coefs):
    return pl.pallas_call(
        owner_kernel,
        out_shape=[
            jax.ShapeDtypeStruct((DEVICES, 128), F32),
            jax.ShapeDtypeStruct((GROUP, 128), F32),
            jax.ShapeDtypeStruct((16, POS), I32),
        ],
        scratch_shapes=[
            pltpu.VMEM((4, 128, POS), F32),
            pltpu.VMEM((GROUP, POS), F32),
            pltpu.VMEM((GROUP, GROUP, 128), F32),
            pltpu.VMEM((GROUP, GROUP, 128), F32),
            pltpu.VMEM((POS, 128), F32),
            pltpu.VMEM((DEVICES, 128), F32),
        ],
        compiler_params=params(WIDE),
        name="owner_work",
    )(rows, coefs)


def coefs_kernel(rows, coefs, steps, lines, out, held):
    unpack(rows, held)
    mem = lines[0:1, :]
    by_rank = onehot((iota((GROUP, POS), 0) == lines[8:9, :]) & (mem >= 0))
    by_member = onehot((iota((128, POS), 0) % MEM) == mem)
    line = jnp.sum(
        by_rank * dot_left(steps[...] * 0.25, by_member.astype(BF16), 2), axis=0, keepdims=True
    )
    weighted = split(by_member[0:MEM, :] * line, 2)
    feats = split(held[...], 2)
    moved = dot(weighted[0], feats[0]) + dot(weighted[0], feats[1]) + dot(weighted[1], feats[0])
    out[...] = 0.25 * coefs[...] - moved


def new_coefs(rows, coefs, steps, lines):
    return pl.pallas_call(
        coefs_kernel,
        out_shape=jax.ShapeDtypeStruct((MEM, 128), F32),
        scratch_shapes=[pltpu.VMEM((POS, 128), F32)],
        compiler_params=params(16),
        name="new_coefs",
    )(rows, coefs, steps, lines)


def total_kernel(back, slots, out):
    slot = slots[...]
    mask = onehot(iota((DEVICES, OWN), 0) == slot // CAP).astype(BF16)
    moved = dot_left(back[...].T, mask, 2)
    keep = (iota((128, OWN), 0) % CAP) == slot % CAP
    out[...] = jnp.sum(jnp.where(keep, moved, 0.0), axis=0, keepdims=True)


def total_rows(back, slots):
    return pl.pallas_call(
        total_kernel,
        out_shape=jax.ShapeDtypeStruct((1, OWN), F32),
        compiler_params=params(16),
        name="total_rows",
    )(back, slots)


def ring_feature(value):
    pairs = [[(i, (i + k) % FEATURES) for i in range(FEATURES)] for k in range(FEATURES)]
    return [value] + [lax.ppermute(value, "feature", pairs[k]) for k in RING[1:]]


def sample_pairs(shift, first):
    pairs = []
    for i in range(SAMPLES):
        x, z, core = i // 8, (i // 2) % 4, i % 2
        if (core == 0) == first:
            z = (z + shift) % 4
        else:
            x = (x + shift) % 4
        pairs.append((i, (x * 4 + z) * 2 + core))
    return pairs


def gather_sample(value):
    early = jnp.concatenate(
        [value] + [lax.ppermute(value, "sample", sample_pairs(k, True)) for k in (1, 2, 3)], axis=0
    )
    late = [early] + [lax.ppermute(early, "sample", sample_pairs(k, False)) for k in (1, 2, 3)]
    return late + [lax.ppermute(v, "sample", [(i, i ^ 1) for i in range(SAMPLES)]) for v in late]


def exchange(value):
    return lax.all_to_all(value, ("sample", "feature"), split_axis=0, concat_axis=0, tiled=True)


def shards(
    feat_values,
    block_ids,
    fixed_weights,
    labels,
    prior_scores,
    member_feats,
    member_ids,
    member_coefs,
):
    members = member_ids.reshape(4, TILE)
    label_tiles = labels.reshape(TILES, TILE)
    prior_tiles = prior_scores.reshape(TILES, TILE)
    margin, chosen, own_ids, sent_ids, merge = first_margin(
        block_ids.T, members, feat_values, fixed_weights
    )
    margins = ring_feature(margin)
    packet = own_stats(margins, prior_tiles, label_tiles, sent_ids, merge, feat_values)
    margin, packet = lax.optimization_barrier((margin, packet))
    packed, slot_row = pack_rows(margin, members, label_tiles, member_feats)
    pieces = gather_sample(packet)
    message = second_margin(pieces, own_ids, chosen, margins, packed, feat_values)
    rows = exchange(message.reshape(DEVICES, 1, NOTE * 128)).reshape(DEVICES * NOTE, 128)
    weights = all_weights(pieces, fixed_weights)
    rows, weights = lax.optimization_barrier((rows, weights))
    back, steps, lines = owner_work(rows, member_coefs)
    returned = exchange(back[:, None, :])[:, 0, :]
    coefs = new_coefs(rows, member_coefs, steps, lines)
    total = total_rows(returned, slot_row)
    return (weights, coefs, total.reshape(OWN, 1))


def solution(mesh):
    both = ("sample", "feature")
    in_specs = (
        P("sample", "feature"),
        P("sample", "feature"),
        P("feature", None),
        P("sample"),
        P("sample"),
        P(both, None),
        P(both),
        P(both, None),
    )
    out_specs = (P("feature", None), P(both, None), P(both, None))
    return jax.shard_map(shards, mesh=mesh, in_specs=in_specs, out_specs=out_specs, check_vma=False)
```

```python
import functools

import jax
import jax.numpy as jnp
from jax import lax
from jax.experimental import pallas as pl
from jax.experimental.pallas import tpu as pltpu
from jax.sharding import PartitionSpec as P

STEP_SIZE = 0.5
FIXED_RIDGE = 0.1
MEMBER_RIDGE = 1.0
MEMBER_STEP = 0.5

F32 = jnp.float32
BF16 = jnp.bfloat16
I32 = jnp.int32

TILES = 16
SLOTS = 4
TILE = 128
BLK = 128
ENTRIES = TILES * SLOTS
PACKET = ENTRIES + 8
DEVICES = 128
SAMPLES = 32
FEATURES = 4
CAP = 8
OWN = 512
POS = DEVICES * CAP
NOTE = CAP + 1
MEM = 32
GROUP = 32
PIVOTS = 4
RING = (0, 1, 3, 2)

NN = (((1,), (0,)), ((), ()))
NT = (((1,), (1,)), ((), ()))


def split(x, parts):
    out = []
    for _ in range(parts - 1):
        top = x.astype(BF16)
        out.append(top)
        x = x - top.astype(F32)
    out.append(x.astype(BF16))
    return out


def dot(a, b, dims=NN):
    return lax.dot_general(a, b, dims, preferred_element_type=F32)


def dot_right(mask, x, parts, dims=NN):
    return functools.reduce(jnp.add, [dot(mask, piece, dims) for piece in split(x, parts)])


def dot_left(x, mask, parts, dims=NN):
    return functools.reduce(jnp.add, [dot(piece, mask, dims) for piece in split(x, parts)])


def iota(shape, dim):
    return lax.broadcasted_iota(I32, shape, dim)


def onehot(cond):
    return jnp.where(cond, 1.0, 0.0).astype(F32)


def params(mib):
    return pltpu.CompilerParams(vmem_limit_bytes=mib << 20)


HBM = pl.BlockSpec(memory_space=pltpu.HBM)
ANY = pl.BlockSpec(memory_space=pl.ANY)
VMEM = pl.BlockSpec(memory_space=pltpu.VMEM)
SMEM = pl.BlockSpec(memory_space=pltpu.SMEM)
CHUNKS = 8
WIDE = 50


def fetch(source, target, sems, chunks=CHUNKS):
    rows = source.shape[0] // chunks
    copies = [
        pltpu.make_async_copy(
            source.at[pl.ds(i * rows, rows)], target.at[pl.ds(i * rows, rows)], sems.at[i]
        )
        for i in range(chunks)
    ]
    for copy in copies:
        copy.start()
    return copies


def tile_margin(feats, weights, t):
    total = None
    for k in range(SLOTS):
        x = feats[t * TILE : (t + 1) * TILE, k * BLK : (k + 1) * BLK]
        e = t * SLOTS + k
        term = x * weights[e : e + 1, :]
        total = term if total is None else total + term
    return total


def margin_kernel(
    ids, members, feats, weights, out, chosen, held, table, own, sums, small_sems, row_sems, sems
):
    early = [
        pltpu.make_async_copy(ids, table, small_sems.at[0]),
        pltpu.make_async_copy(members, own, small_sems.at[1]),
    ]
    for copy in early:
        copy.start()
    copies = fetch(feats, held, sems)
    early[0].wait()
    picked = [
        pltpu.make_async_copy(
            weights.at[pl.ds(table[e % SLOTS, e // SLOTS], 1)],
            chosen.at[pl.ds(e, 1)],
            row_sems.at[e],
        )
        for e in range(ENTRIES)
    ]
    for copy in picked:
        copy.start()
    early[1].wait()

    owner = own[...] // MEM
    column = owner.astype(F32).T.astype(I32)
    sub, lane = iota((TILE, TILE), 0), iota((TILE, TILE), 1)
    for a in range(4):
        rank = None
        for b in range(a + 1):
            same = jnp.broadcast_to(column[:, b : b + 1], (TILE, TILE)) == owner[a : a + 1, :]
            if a == b:
                same = same & (sub < lane)
            term = jnp.sum(onehot(same), axis=0, keepdims=True)
            rank = term if rank is None else rank + term
        out[TILES + a : TILES + a + 1, :] = owner[a : a + 1, :].astype(F32) * CAP + rank
    out[TILES + 4 :, :] = jnp.zeros((4, TILE), F32)

    for copy in picked:
        copy.wait()
    each = TILES // CHUNKS
    for c in range(CHUNKS):
        copies[c].wait()
        for t in range(c * each, (c + 1) * each):
            sums[t * TILE : (t + 1) * TILE, :] = tile_margin(held, chosen, t)
    for t in range(TILES):
        across = sums[t * TILE : (t + 1) * TILE, :].T
        out[t : t + 1, :] = jnp.sum(across, axis=0, keepdims=True)


def first_margin(ids, members, feats, weights):
    return pl.pallas_call(
        margin_kernel,
        in_specs=[HBM, HBM, HBM, HBM],
        out_shape=[
            jax.ShapeDtypeStruct((TILES + 8, TILE), F32),
            jax.ShapeDtypeStruct((ENTRIES, BLK), F32),
            pltpu.VMEM(feats.shape, F32),
        ],
        scratch_shapes=[
            pltpu.SMEM(ids.shape, I32),
            pltpu.VMEM(members.shape, I32),
            pltpu.VMEM((TILES * TILE, BLK), F32),
            pltpu.SemaphoreType.DMA((2,)),
            pltpu.SemaphoreType.DMA((ENTRIES,)),
            pltpu.SemaphoreType.DMA((CHUNKS,)),
        ],
        compiler_params=params(47),
        name="first_margin",
    )(ids, members, feats, weights)


def table_kernel(ids, limit, own, sent, merge):
    at, of = iota((ENTRIES, 128), 0), iota((ENTRIES, 128), 1) % ENTRIES
    rows = jnp.zeros((ENTRIES, 128), I32)
    line = jnp.zeros((8, 128), I32)
    for e in range(ENTRIES):
        block = ids[e % SLOTS, e // SLOTS]
        rows = jnp.where(at == e, block, rows)
        line = jnp.where(of[0:8, :] == e, block, line)
    same = rows == line[0:1, :]
    repeat = jnp.sum(onehot(same & (at < of)), axis=0, keepdims=True)
    own[...] = rows.astype(F32)
    kept = jnp.where(repeat > 0.0, limit, line[0:1, :]).astype(F32)
    sent[...] = jnp.broadcast_to(jnp.concatenate([kept, kept], axis=1), (8, 256))
    earlier = jnp.sum(onehot(same & (of < at)), axis=1, keepdims=True)
    merge[...] = jnp.where(earlier > 0.0, 0.0, onehot(same))


def block_tables(ids, limit):
    def kernel(ids, *refs):
        table_kernel(ids, limit, *refs)

    table = jax.ShapeDtypeStruct((ENTRIES, BLK), F32)
    return pl.pallas_call(
        kernel,
        in_specs=[SMEM],
        out_shape=[table, jax.ShapeDtypeStruct((8, 2 * BLK), F32), table],
        compiler_params=params(16),
        name="block_tables",
    )(ids)


def stats_kernel(m0, m1, m2, m3, prior, labels, ids, merge, held, out, raw):
    margin = (m0[0:TILES, :] + m1[0:TILES, :]) + (m2[0:TILES, :] + m3[0:TILES, :])
    probs = jax.nn.sigmoid(margin + prior[...])
    residual = (probs - labels[...]).T
    curvature = (probs * (1.0 - probs)).T
    for t in range(TILES):
        r = jnp.broadcast_to(residual[:, t : t + 1], (TILE, BLK))
        c = jnp.broadcast_to(curvature[:, t : t + 1], (TILE, BLK))
        for k in range(SLOTS):
            x = held[t * TILE : (t + 1) * TILE, k * BLK : (k + 1) * BLK]
            e = t * SLOTS + k
            raw[e : e + 1, 0:BLK] = jnp.sum(x * r, axis=0, keepdims=True)
            raw[e : e + 1, BLK : 2 * BLK] = jnp.sum(x * x * c, axis=0, keepdims=True)
    out[0:ENTRIES, :] = dot_right(merge[:, 0:ENTRIES].astype(BF16), raw[...], 3)
    out[ENTRIES:PACKET, :] = ids[...]


def own_stats(margins, prior, labels, ids, merge, feats):
    return pl.pallas_call(
        stats_kernel,
        in_specs=[VMEM] * 9,
        out_shape=jax.ShapeDtypeStruct((PACKET, 2 * BLK), F32),
        scratch_shapes=[
            pltpu.VMEM((ENTRIES, 2 * BLK), F32),
        ],
        compiler_params=params(16),
        name="own_stats",
    )(*margins, prior, labels, ids, merge, feats)


def sum_pieces(own_ids, pieces):
    lane = iota((1, 128), 1)
    acc = None
    for piece in pieces:
        for a in (0, 2 * PACKET):
            b = a + PACKET
            ids = jnp.where(
                lane < ENTRIES,
                piece[a + ENTRIES : a + ENTRIES + 1, 0:128],
                piece[b + ENTRIES : b + ENTRIES + 1, 0:128],
            )
            mask = onehot(own_ids[...] == ids).astype(BF16)
            both = jnp.concatenate([piece[a : a + ENTRIES, :], piece[b : b + ENTRIES, :]], axis=0)
            term = dot_right(mask, both, 2)
            acc = term if acc is None else acc + term
    return acc


def near_kernel(own_ids, *rest):
    pieces, out = rest[:4], rest[4]
    out[...] = sum_pieces(own_ids, pieces)


def near_sums(own_ids, pieces):
    return pl.pallas_call(
        near_kernel,
        out_shape=jax.ShapeDtypeStruct((ENTRIES, 2 * BLK), F32),
        compiler_params=params(16),
        name="near_sums",
    )(own_ids, *pieces)


def second_kernel(own_ids, chosen, packed, near, feats, *rest):
    margins, pieces, (out, slots) = rest[:4], rest[4:8], rest[8:]
    acc = near[...] + sum_pieces(own_ids, pieces)
    w = chosen[...]
    w = w - STEP_SIZE * (acc[:, :BLK] + FIXED_RIDGE * w) / (acc[:, BLK:] + 1.0)
    ones = jnp.ones((BLK, 128), BF16)
    feature = lax.axis_index("feature")
    for shift, margin in zip(RING, margins):
        source = lax.rem(feature + FEATURES - shift, FEATURES)
        slots[pl.ds(source * 4, 4), :] = margin[TILES : TILES + 4, :]
    slot = slots[...].astype(I32)
    column = (slot % CAP + CAP * (iota((TILES, TILE), 0) // 4)).astype(F32).T
    owner = slot // CAP
    result = None
    lanes = (iota((TILE, 128), 1) % 32).astype(F32)
    for t in range(0, TILES, 2):
        both = [tile_margin(feats, w, t), tile_margin(feats, w, t + 1)]
        margin = dot_left(jnp.concatenate(both, axis=0), ones, 2)
        place = [
            lanes == jnp.broadcast_to(column[:, q : q + 1], (TILE, 128)) for q in (t, t + 1)
        ]
        placed = jnp.where(jnp.concatenate(place, axis=0), margin, 0.0)
        owners = jnp.concatenate([owner[t : t + 1, :], owner[t + 1 : t + 2, :]], axis=1)
        mask = onehot(iota((DEVICES, 2 * TILE), 0) == owners).astype(BF16)
        term = dot_right(mask, placed, 2)
        result = term if result is None else result + term
    out[...] = packed[...]
    result = jnp.where(iota((DEVICES, 128), 1) < 32, result, 0.0)
    for d in range(DEVICES):
        at = NOTE * d + CAP
        out[at : at + 1, :] = packed[at : at + 1, :] + result[d : d + 1, :]


def second_margin(near, pieces, own_ids, chosen, margins, packed, feats):
    return pl.pallas_call(
        second_kernel,
        in_specs=[VMEM] * 13,
        out_shape=jax.ShapeDtypeStruct((DEVICES * NOTE, 128), F32),
        scratch_shapes=[
            pltpu.VMEM((TILES, TILE), F32),
        ],
        compiler_params=params(16),
        name="second_margin",
    )(own_ids, chosen, packed, near, feats, *margins, *pieces)


def gathered_place(source):
    me = lax.axis_index("sample")
    x, z, core = me // 8, (me // 2) % 4, me % 2
    xs, zs, cs = source // 8, (source // 2) % 4, source % 2
    along_x, along_z = (x - xs + 4) % 4, (z - zs + 4) % 4
    late = jnp.where(cs == 0, along_x, along_z)
    early = jnp.where(cs == 0, along_z, along_x)
    return jnp.where(cs == core, 0, 16) + late * 4 + early


def weights_kernel(weights, *rest):
    pieces, rest = rest[:8], rest[8:]
    out, held, grad, hess, sent, table, ids, in_sems, out_sems, piece_sems, id_sem = rest
    blocks = weights.shape[0]
    arrivals = [
        pltpu.make_async_copy(piece, sent.at[pl.ds(4 * PACKET * i, 4 * PACKET)], piece_sems.at[i])
        for i, piece in enumerate(pieces)
    ]
    for copy in arrivals:
        copy.start()
    copies = fetch(weights, held, in_sems)

    def clear(i, carry):
        at = pl.ds(pl.multiple_of(i * 256, 256), 256)
        grad[at, :] = jnp.zeros((256, BLK), F32)
        hess[at, :] = jnp.zeros((256, BLK), F32)
        return carry

    lax.fori_loop(0, blocks // 256, clear, 0)
    for copy in arrivals:
        copy.wait()

    lines = [sent[i * PACKET + ENTRIES : i * PACKET + ENTRIES + 1, 0:128] for i in range(SAMPLES)]
    table[...] = jnp.concatenate(lines, axis=0).astype(I32)
    copy = pltpu.make_async_copy(table, ids, id_sem)
    copy.start()
    copy.wait()

    def source(s, carry):
        at = gathered_place(s)
        packet = sent.at[pl.ds(pl.multiple_of(at * PACKET, 8), PACKET)]
        for first in range(0, ENTRIES, 16):
            span = range(first, first + 16)
            rows = [pl.ds(ids[at, j], 1) for j in span]
            old = [(grad[r, :], hess[r, :]) for r in rows]
            new = [
                (g + packet[j : j + 1, 0:BLK], h + packet[j : j + 1, BLK : 2 * BLK])
                for j, (g, h) in zip(span, old)
            ]
            for r, (g, h) in zip(rows, new):
                grad[r, :] = g
                hess[r, :] = h
        return carry

    lax.fori_loop(0, SAMPLES, source, 0)
    size = blocks // CHUNKS
    done = []
    for c in range(CHUNKS):
        copies[c].wait()

        def update(i, carry, c=c):
            at = pl.ds(pl.multiple_of(c * size + i * 256, 256), 256)
            w = held[at, :]
            held[at, :] = w - STEP_SIZE * (grad[at, :] + FIXED_RIDGE * w) / (hess[at, :] + 1.0)
            return carry

        lax.fori_loop(0, size // 256, update, 0)
        at = pl.ds(c * size, size)
        copy = pltpu.make_async_copy(held.at[at], out.at[at], out_sems.at[c])
        copy.start()
        done.append(copy)
    for copy in done:
        copy.wait()


def all_weights(pieces, weights):
    blocks = weights.shape[0]
    return pl.pallas_call(
        weights_kernel,
        in_specs=[HBM] + [ANY] * 8,
        out_specs=HBM,
        out_shape=jax.ShapeDtypeStruct((blocks, BLK), F32),
        scratch_shapes=[
            pltpu.VMEM((blocks, BLK), F32),
            pltpu.VMEM((blocks + 8, BLK), F32),
            pltpu.VMEM((blocks + 8, BLK), F32),
            pltpu.VMEM((SAMPLES * PACKET, 2 * BLK), F32),
            pltpu.VMEM((SAMPLES, 128), I32),
            pltpu.SMEM((SAMPLES, 128), I32),
            pltpu.SemaphoreType.DMA((CHUNKS,)),
            pltpu.SemaphoreType.DMA((CHUNKS,)),
            pltpu.SemaphoreType.DMA((8,)),
            pltpu.SemaphoreType.DMA,
        ],
        compiler_params=params(WIDE),
        name="all_weights",
    )(weights, *pieces)


def pack_kernel(margin, members, labels, feats, out, slot, placed):
    feature = lax.axis_index("feature")
    slots = margin[TILES : TILES + 4, :].astype(I32)
    own = labels[pl.ds(feature * 4, 4), :]
    local = (members[...] % MEM + 1).astype(F32)
    columns = jnp.concatenate([(slots % CAP).astype(F32), own, local], axis=0).T
    lane = iota((TILE, 128), 1)
    within = (lane % CAP).astype(F32)
    for a in range(4):
        slot[:, a * TILE : (a + 1) * TILE] = slots[a : a + 1, :]
        rank, label, member = (
            jnp.broadcast_to(columns[:, 4 * q + a : 4 * q + a + 1], (TILE, 128)) for q in range(3)
        )
        value = jnp.where(lane // CAP == 4, label, jnp.where(lane // CAP == 5, member, 0.0))
        placed[a * TILE : (a + 1) * TILE, :] = jnp.where(within == rank, value, 0.0)
    line = slot[...]
    rows = dot_right(onehot(iota((POS, OWN), 0) == line).astype(BF16), feats[...], 3)
    notes = dot_right(onehot(iota((DEVICES, OWN), 0) == line // CAP).astype(BF16), placed[...], 3)
    for d in range(DEVICES):
        out[NOTE * d : NOTE * d + CAP, :] = rows[CAP * d : CAP * (d + 1), :]
        out[NOTE * d + CAP : NOTE * (d + 1), :] = notes[d : d + 1, :]


def pack_rows(margin, members, labels, feats):
    return pl.pallas_call(
        pack_kernel,
        out_shape=[
            jax.ShapeDtypeStruct((DEVICES * NOTE, 128), F32),
            jax.ShapeDtypeStruct((1, OWN), I32),
        ],
        scratch_shapes=[pltpu.VMEM((OWN, 128), F32)],
        compiler_params=params(16),
        name="pack_rows",
    )(margin, members, labels, feats)


def gram_times(gram, v):
    out = None
    for i in range(GROUP):
        term = gram[i] * v[i : i + 1, :]
        out = term if out is None else out + term
    return out


def spread(block, source):
    group = iota(block.shape, 1) // MEM
    out = None
    for g in range(4):
        shift = (g - source) % 4
        moved = pltpu.roll(block, MEM * shift, 1) if shift else block
        out = moved if out is None else jnp.where(group == g, moved, out)
    return out


def unpack(rows, feats, notes=None):
    for d in range(DEVICES):
        feats[CAP * d : CAP * (d + 1), :] = rows[NOTE * d : NOTE * d + CAP, :]
        if notes is not None:
            notes[d : d + 1, :] = rows[NOTE * d + CAP : NOTE * (d + 1), :]


def repeat_lanes(x, first, size):
    lane = iota(x.shape, 1)
    x = jnp.where((lane >= first) & (lane < first + size), x, 0.0)
    while size < 128:
        x = x + pltpu.roll(x, size, 1)
        size *= 2
    return x


def owner_kernel(rows, coefs, back, steps, lines, turned, diag, gram, work, held, notes):
    unpack(rows, held, notes)
    sub, lane = iota((128, 128), 0), iota((128, 128), 1)
    lab_parts, mem_parts, fixed_parts = [], [], []
    labs = repeat_lanes(notes[...], 4 * CAP, CAP)
    mems = repeat_lanes(notes[...], 5 * CAP, CAP)
    got = repeat_lanes(notes[...], 0, 32)
    for b in range(8):
        at = slice(16 * b, 16 * (b + 1))
        keep = iota((16, 128), 0) == iota((16, 128), 1) // CAP
        lab_parts.append(jnp.sum(jnp.where(keep, labs[at, :], 0.0), axis=0, keepdims=True))
        mem_parts.append(jnp.sum(jnp.where(keep, mems[at, :], 0.0), axis=0, keepdims=True))
        keep = iota((16, 128), 0) // FEATURES == iota((16, 128), 1) // 32
        fixed_parts.append(jnp.sum(jnp.where(keep, got[at, :], 0.0), axis=0, keepdims=True))
    lab = jnp.concatenate(lab_parts, axis=1)
    fixed = jnp.concatenate(fixed_parts, axis=1)
    mem = jnp.concatenate(mem_parts, axis=1).astype(I32) - 1
    few = onehot(iota((MEM, POS), 0) == mem)
    before = onehot(sub < lane).astype(BF16)
    ones = jnp.ones((128, 128), BF16)
    carry = jnp.zeros((MEM, 128), F32)
    ranks = []
    for b in range(8):
        part = few[:, 128 * b : 128 * (b + 1)]
        half = part.astype(BF16)
        count = dot(half, before) + carry
        carry = carry + dot(half, ones)
        ranks.append(jnp.sum(part * count, axis=0, keepdims=True))
    rnk = jnp.concatenate(ranks, axis=1).astype(I32)
    lines[0:8, :] = jnp.broadcast_to(mem, (8, POS))
    lines[8:16, :] = jnp.broadcast_to(rnk, (8, POS))
    by_rank = onehot((iota((GROUP, POS), 0) == rnk) & (mem >= 0))
    by_member = onehot((iota((128, POS), 0) % MEM) == mem).astype(BF16)
    y = dot_left(by_rank * lab, by_member, 3, NT)
    offset = dot_left(by_rank * fixed, by_member, 2, NT)
    alive = dot(by_rank.astype(BF16), by_member, NT)
    target = jnp.where(mem >= 0, rnk * MEM + mem, -1)
    feats = held[...].T
    pieces = jnp.concatenate(split(feats, 2), axis=0)
    for b in range(4):
        goal = onehot(iota((256, POS), 0) + 256 * b == target).astype(BF16)
        moved = dot(pieces, goal, NT)
        turned[0, :, 256 * b : 256 * (b + 1)] = moved[0:128, :] + moved[128:256, :]
    x = turned[0]
    for p in range(1, 4):
        turned[p] = pltpu.roll(x, POS - MEM * p, 1)
    c = jnp.concatenate([coefs[...]] * 4, axis=0).T
    own = jnp.sum(x * jnp.concatenate([c] * 8, axis=1), axis=0, keepdims=True)
    own = jnp.where(iota((GROUP, POS), 1) // MEM == iota((GROUP, POS), 0), own, 0.0)
    folded = own[:, 0:128]
    for b in range(1, 8):
        folded = folded + own[:, 128 * b : 128 * (b + 1)]
    folded = folded + pltpu.roll(folded, 64, 1)
    s = folded + pltpu.roll(folded, 32, 1)
    for delta in range(GROUP // 2 + 1):
        p, q = delta % 4, delta // 4
        for b in range(8):
            o = (b + q) % 8
            prod = turned[0, :, 128 * b : 128 * (b + 1)] * turned[p, :, 128 * o : 128 * (o + 1)]
            diag[delta : delta + 1, 128 * b : 128 * (b + 1)] = jnp.sum(prod, axis=0, keepdims=True)
    for delta in range(GROUP // 2 + 1, GROUP):
        diag[delta : delta + 1, :] = pltpu.roll(
            jnp.broadcast_to(diag[GROUP - delta : GROUP - delta + 1, :], (8, POS)), POS - MEM * delta, 1
        )[0:1, :]
    for b in range(8):
        block = diag[:, 128 * b : 128 * (b + 1)]
        for p in range(4):
            i = 4 * b + p
            wide = spread(block, p)
            gram[i] = pltpu.roll(wide, i, 0) if i else wide
    at = iota((GROUP, 128), 0)
    steps_total = None
    for sweep in range(2):
        p = jax.nn.sigmoid(s + offset)
        error = (p - y) * alive
        d = jnp.sqrt(p * (1.0 - p) * alive)
        b = d * (gram_times(gram, error) + s)
        for i in range(GROUP):
            row = gram[i] * (d * d[i : i + 1, :])
            work[i] = row + onehot(at == i)
        for k in range(0, GROUP, PIVOTS):
            panel = [work[k + q] for q in range(PIVOTS)]
            taken = []
            for q in range(PIVOTS):
                row = panel[q]
                inverse = 1.0 / row[k + q : k + q + 1, :]
                scaled = jnp.where(at == k + q, 1.0 - inverse, row * inverse)
                for r in range(q + 1, PIVOTS):
                    panel[r] = panel[r] - row[k + r : k + r + 1, :] * scaled
                b = b - b[k + q : k + q + 1, :] * scaled
                taken.append((row, scaled))
            for i in range(k + PIVOTS, GROUP):
                rest = work[i]
                for row, scaled in taken:
                    rest = rest - row[i : i + 1, :] * scaled
                work[i] = rest
        u = error - d * b
        s = s - MEMBER_STEP * (gram_times(gram, u) + MEMBER_RIDGE * s)
        steps_total = u * 0.25 if sweep == 0 else steps_total + u * 0.5
    steps[...] = steps_total
    final = (s + offset) * 0.25
    scores = jnp.sum(by_rank * dot_left(final, by_member, 2), axis=0, keepdims=True)
    for b in range(8):
        line = jnp.broadcast_to(scores[:, 128 * b : 128 * (b + 1)], (16, 128))
        back[16 * b : 16 * (b + 1), :] = jnp.where(
            iota((16, 128), 1) // CAP == iota((16, 128), 0), line, 0.0
        )


def owner_work(rows, coefs):
    return pl.pallas_call(
        owner_kernel,
        out_shape=[
            jax.ShapeDtypeStruct((DEVICES, 128), F32),
            jax.ShapeDtypeStruct((GROUP, 128), F32),
            jax.ShapeDtypeStruct((16, POS), I32),
        ],
        scratch_shapes=[
            pltpu.VMEM((4, 128, POS), F32),
            pltpu.VMEM((GROUP, POS), F32),
            pltpu.VMEM((GROUP, GROUP, 128), F32),
            pltpu.VMEM((GROUP, GROUP, 128), F32),
            pltpu.VMEM((POS, 128), F32),
            pltpu.VMEM((DEVICES, 128), F32),
        ],
        compiler_params=params(WIDE),
        name="owner_work",
    )(rows, coefs)


def coefs_kernel(rows, coefs, steps, lines, out, held):
    unpack(rows, held)
    mem = lines[0:1, :]
    by_rank = onehot((iota((GROUP, POS), 0) == lines[8:9, :]) & (mem >= 0))
    by_member = onehot((iota((128, POS), 0) % MEM) == mem)
    line = jnp.sum(
        by_rank * dot_left(steps[...] * 0.25, by_member.astype(BF16), 2), axis=0, keepdims=True
    )
    weighted = split(by_member[0:MEM, :] * line, 2)
    feats = split(held[...], 2)
    moved = dot(weighted[0], feats[0]) + dot(weighted[0], feats[1]) + dot(weighted[1], feats[0])
    out[...] = 0.25 * coefs[...] - moved


def new_coefs(rows, coefs, steps, lines):
    return pl.pallas_call(
        coefs_kernel,
        out_shape=jax.ShapeDtypeStruct((MEM, 128), F32),
        scratch_shapes=[pltpu.VMEM((POS, 128), F32)],
        compiler_params=params(16),
        name="new_coefs",
    )(rows, coefs, steps, lines)


def total_kernel(back, slots, out):
    slot = slots[...]
    mask = onehot(iota((DEVICES, OWN), 0) == slot // CAP).astype(BF16)
    moved = dot_left(back[...].T, mask, 2)
    keep = (iota((128, OWN), 0) % CAP) == slot % CAP
    out[...] = jnp.sum(jnp.where(keep, moved, 0.0), axis=0, keepdims=True)


def total_rows(back, slots):
    return pl.pallas_call(
        total_kernel,
        out_shape=jax.ShapeDtypeStruct((1, OWN), F32),
        compiler_params=params(16),
        name="total_rows",
    )(back, slots)


def ring_feature(value):
    pairs = [[(i, (i + k) % FEATURES) for i in range(FEATURES)] for k in range(FEATURES)]
    return [value] + [lax.ppermute(value, "feature", pairs[k]) for k in RING[1:]]


def sample_pairs(shift, first):
    pairs = []
    for i in range(SAMPLES):
        x, z, core = i // 8, (i // 2) % 4, i % 2
        if (core == 0) == first:
            z = (z + shift) % 4
        else:
            x = (x + shift) % 4
        pairs.append((i, (x * 4 + z) * 2 + core))
    return pairs


def join_kernel(*refs):
    out = refs[-1]
    for i, ref in enumerate(refs[:-1]):
        out[i * PACKET : (i + 1) * PACKET, :] = ref[...]


def join(packets):
    return pl.pallas_call(
        join_kernel,
        out_shape=jax.ShapeDtypeStruct((len(packets) * PACKET, 2 * BLK), F32),
        compiler_params=params(16),
        name="join",
    )(*packets)


def gather_early(value):
    return join([value] + [lax.ppermute(value, "sample", sample_pairs(k, True)) for k in (1, 2, 3)])


def gather_late(early):
    late = [early] + [lax.ppermute(early, "sample", sample_pairs(k, False)) for k in (1, 2, 3)]
    other = [lax.ppermute(v, "sample", [(i, i ^ 1) for i in range(SAMPLES)]) for v in late]
    return late, other


def exchange(value):
    return lax.all_to_all(value, ("sample", "feature"), split_axis=0, concat_axis=0, tiled=True)


def shards(
    feat_values,
    block_ids,
    fixed_weights,
    labels,
    prior_scores,
    member_feats,
    member_ids,
    member_coefs,
):
    members = member_ids.reshape(4, TILE)
    label_tiles = labels.reshape(TILES, TILE)
    prior_tiles = prior_scores.reshape(TILES, TILE)
    ids = block_ids.T
    margin, chosen, held = first_margin(
        pltpu.with_memory_space_constraint(ids, pltpu.HBM),
        pltpu.with_memory_space_constraint(members, pltpu.HBM),
        feat_values,
        fixed_weights,
    )
    margin, ids = lax.optimization_barrier((margin, ids))
    own_ids, sent_ids, merge = block_tables(ids, fixed_weights.shape[0])
    margins = ring_feature(margin)
    packet = own_stats(margins, prior_tiles, label_tiles, sent_ids, merge, held)
    margin, packet = lax.optimization_barrier((margin, packet))
    packed, slot_row = pack_rows(margin, members, label_tiles, member_feats)
    early = gather_early(packet)
    early, packed = lax.optimization_barrier((early, packed))
    late, other = gather_late(early)
    near = near_sums(own_ids, late)
    message = second_margin(near, other, own_ids, chosen, margins, packed, held)
    rows = exchange(message.reshape(DEVICES, 1, NOTE * 128)).reshape(DEVICES * NOTE, 128)
    pieces = late + other
    weights = all_weights(pieces, fixed_weights)
    rows, weights = lax.optimization_barrier((rows, weights))
    back, steps, lines = owner_work(rows, member_coefs)
    returned = exchange(back[:, None, :])[:, 0, :]
    coefs = new_coefs(rows, member_coefs, steps, lines)
    total = total_rows(returned, slot_row)
    return (weights, coefs, total.reshape(OWN, 1))


def solution(mesh):
    both = ("sample", "feature")
    in_specs = (
        P("sample", "feature"),
        P("sample", "feature"),
        P("feature", None),
        P("sample"),
        P("sample"),
        P(both, None),
        P(both),
        P(both, None),
    )
    out_specs = (P("feature", None), P(both, None), P(both, None))
    return jax.shard_map(shards, mesh=mesh, in_specs=in_specs, out_specs=out_specs, check_vma=False)
```

```python
import functools

import jax
import jax.numpy as jnp
from jax import lax
from jax.experimental import pallas as pl
from jax.experimental.pallas import tpu as pltpu
from jax.sharding import PartitionSpec as P

STEP_SIZE = 0.5
FIXED_RIDGE = 0.1
MEMBER_RIDGE = 1.0
MEMBER_STEP = 0.5

F32 = jnp.float32
BF16 = jnp.bfloat16
I32 = jnp.int32

TILES = 16
SLOTS = 4
TILE = 128
BLK = 128
ENTRIES = TILES * SLOTS
PACKET = ENTRIES + 8
DEVICES = 128
SAMPLES = 32
FEATURES = 4
CAP = 8
OWN = 512
POS = DEVICES * CAP
NOTE = CAP + 1
MEM = 32
GROUP = 32
PIVOTS = 4
RING = (0, 1, 3, 2)

NN = (((1,), (0,)), ((), ()))
NT = (((1,), (1,)), ((), ()))


def split(x, parts):
    out = []
    for _ in range(parts - 1):
        top = x.astype(BF16)
        out.append(top)
        x = x - top.astype(F32)
    out.append(x.astype(BF16))
    return out


def dot(a, b, dims=NN):
    return lax.dot_general(a, b, dims, preferred_element_type=F32)


def dot_right(mask, x, parts):
    return dot(jnp.concatenate([mask] * parts, axis=1), jnp.concatenate(split(x, parts), axis=0))


def dot_left(values, mask, dims=NN):
    pieces = [piece for x, parts in values for piece in split(x, parts)]
    out = dot(jnp.concatenate(pieces, axis=0), mask, dims)
    results, at = [], 0
    for x, parts in values:
        rows = x.shape[0]
        results.append(
            sum_pieces_of([out[at + p * rows : at + (p + 1) * rows, :] for p in range(parts)])
        )
        at += parts * rows
    return results


def sum_pieces_of(pieces):
    return functools.reduce(jnp.add, pieces)


def iota(shape, dim):
    return lax.broadcasted_iota(I32, shape, dim)


def onehot(cond):
    return jnp.where(cond, 1.0, 0.0).astype(F32)


def params(mib):
    return pltpu.CompilerParams(vmem_limit_bytes=mib << 20)


HBM = pl.BlockSpec(memory_space=pltpu.HBM)
ANY = pl.BlockSpec(memory_space=pl.ANY)
VMEM = pl.BlockSpec(memory_space=pltpu.VMEM)
SMEM = pl.BlockSpec(memory_space=pltpu.SMEM)
CHUNKS = 8
WIDE = 50


def fetch(source, target, sems, chunks=CHUNKS):
    rows = source.shape[0] // chunks
    copies = [
        pltpu.make_async_copy(
            source.at[pl.ds(i * rows, rows)], target.at[pl.ds(i * rows, rows)], sems.at[i]
        )
        for i in range(chunks)
    ]
    for copy in copies:
        copy.start()
    return copies


def tile_margin(feats, weights, t):
    total = None
    for k in range(SLOTS):
        x = feats[t * TILE : (t + 1) * TILE, k * BLK : (k + 1) * BLK]
        e = t * SLOTS + k
        term = x * weights[e : e + 1, :]
        total = term if total is None else total + term
    return total


def margin_kernel(
    ids, members, feats, weights, out, chosen, held, table, own, sums, small_sems, row_sems, sems
):
    early = [
        pltpu.make_async_copy(ids, table, small_sems.at[0]),
        pltpu.make_async_copy(members, own, small_sems.at[1]),
    ]
    for copy in early:
        copy.start()
    copies = fetch(feats, held, sems)
    early[0].wait()
    picked = [
        pltpu.make_async_copy(
            weights.at[pl.ds(table[e % SLOTS, e // SLOTS], 1)],
            chosen.at[pl.ds(e, 1)],
            row_sems.at[e],
        )
        for e in range(ENTRIES)
    ]
    for copy in picked:
        copy.start()
    early[1].wait()

    owner = own[...] // MEM
    column = owner.astype(F32).T.astype(I32)
    sub, lane = iota((TILE, TILE), 0), iota((TILE, TILE), 1)
    for a in range(4):
        rank = None
        for b in range(a + 1):
            same = jnp.broadcast_to(column[:, b : b + 1], (TILE, TILE)) == owner[a : a + 1, :]
            if a == b:
                same = same & (sub < lane)
            term = jnp.sum(onehot(same), axis=0, keepdims=True)
            rank = term if rank is None else rank + term
        out[TILES + a : TILES + a + 1, :] = owner[a : a + 1, :].astype(F32) * CAP + rank
    out[TILES + 4 :, :] = jnp.zeros((4, TILE), F32)

    each = TILES // CHUNKS
    for c in range(CHUNKS):
        for copy in picked[c * each * SLOTS : (c + 1) * each * SLOTS]:
            copy.wait()
        copies[c].wait()
        for t in range(c * each, (c + 1) * each):
            sums[t * TILE : (t + 1) * TILE, :] = tile_margin(held, chosen, t)
    for t in range(TILES):
        across = sums[t * TILE : (t + 1) * TILE, :].T
        out[t : t + 1, :] = jnp.sum(across, axis=0, keepdims=True)


def first_margin(ids, members, feats, weights):
    return pl.pallas_call(
        margin_kernel,
        in_specs=[HBM, HBM, HBM, HBM],
        out_shape=[
            jax.ShapeDtypeStruct((TILES + 8, TILE), F32),
            jax.ShapeDtypeStruct((ENTRIES, BLK), F32),
            pltpu.VMEM(feats.shape, F32),
        ],
        scratch_shapes=[
            pltpu.SMEM(ids.shape, I32),
            pltpu.VMEM(members.shape, I32),
            pltpu.VMEM((TILES * TILE, BLK), F32),
            pltpu.SemaphoreType.DMA((2,)),
            pltpu.SemaphoreType.DMA((ENTRIES,)),
            pltpu.SemaphoreType.DMA((CHUNKS,)),
        ],
        compiler_params=params(47),
        name="first_margin",
    )(ids, members, feats, weights)


def table_kernel(ids, limit, own, sent, merge):
    at, of = iota((ENTRIES, 128), 0), iota((ENTRIES, 128), 1) % ENTRIES
    rows = jnp.zeros((ENTRIES, 128), I32)
    line = jnp.zeros((8, 128), I32)
    for e in range(ENTRIES):
        block = ids[e % SLOTS, e // SLOTS]
        rows = jnp.where(at == e, block, rows)
        line = jnp.where(of[0:8, :] == e, block, line)
    same = rows == line[0:1, :]
    repeat = jnp.sum(onehot(same & (at < of)), axis=0, keepdims=True)
    own[...] = rows.astype(F32)
    kept = jnp.where(repeat > 0.0, limit, line[0:1, :]).astype(F32)
    sent[...] = jnp.broadcast_to(jnp.concatenate([kept, kept], axis=1), (8, 256))
    earlier = jnp.sum(onehot(same & (of < at)), axis=1, keepdims=True)
    merge[...] = jnp.where(earlier > 0.0, 0.0, onehot(same))


def block_tables(ids, limit):
    def kernel(ids, *refs):
        table_kernel(ids, limit, *refs)

    table = jax.ShapeDtypeStruct((ENTRIES, BLK), F32)
    return pl.pallas_call(
        kernel,
        in_specs=[SMEM],
        out_shape=[table, jax.ShapeDtypeStruct((8, 2 * BLK), F32), table],
        compiler_params=params(16),
        name="block_tables",
    )(ids)


def stats_kernel(m0, m1, m2, m3, prior, labels, ids, merge, held, out, raw):
    margin = (m0[0:TILES, :] + m1[0:TILES, :]) + (m2[0:TILES, :] + m3[0:TILES, :])
    probs = jax.nn.sigmoid(margin + prior[...])
    residual = (probs - labels[...]).T
    curvature = (probs * (1.0 - probs)).T
    for t in range(TILES):
        r = jnp.broadcast_to(residual[:, t : t + 1], (TILE, BLK))
        c = jnp.broadcast_to(curvature[:, t : t + 1], (TILE, BLK))
        for k in range(SLOTS):
            x = held[t * TILE : (t + 1) * TILE, k * BLK : (k + 1) * BLK]
            e = t * SLOTS + k
            raw[e : e + 1, 0:BLK] = jnp.sum(x * r, axis=0, keepdims=True)
            raw[e : e + 1, BLK : 2 * BLK] = jnp.sum(x * x * c, axis=0, keepdims=True)
    out[0:ENTRIES, :] = dot_right(merge[:, 0:ENTRIES].astype(BF16), raw[...], 3)
    out[ENTRIES:PACKET, :] = ids[...]


def own_stats(margins, prior, labels, ids, merge, feats):
    return pl.pallas_call(
        stats_kernel,
        in_specs=[VMEM] * 9,
        out_shape=jax.ShapeDtypeStruct((PACKET, 2 * BLK), F32),
        scratch_shapes=[
            pltpu.VMEM((ENTRIES, 2 * BLK), F32),
        ],
        compiler_params=params(16),
        name="own_stats",
    )(*margins, prior, labels, ids, merge, feats)


def sum_pieces(own_ids, pieces):
    lane = iota((1, 128), 1)
    acc = None
    for piece in pieces:
        for a in (0, 2 * PACKET):
            b = a + PACKET
            ids = jnp.where(
                lane < ENTRIES,
                piece[a + ENTRIES : a + ENTRIES + 1, 0:128],
                piece[b + ENTRIES : b + ENTRIES + 1, 0:128],
            )
            mask = onehot(own_ids[...] == ids).astype(BF16)
            both = jnp.concatenate([piece[a : a + ENTRIES, :], piece[b : b + ENTRIES, :]], axis=0)
            term = dot_right(mask, both, 2)
            acc = term if acc is None else acc + term
    return acc


def near_kernel(own_ids, *rest):
    pieces, out = rest[:4], rest[4]
    out[...] = sum_pieces(own_ids, pieces)


def near_sums(own_ids, pieces):
    return pl.pallas_call(
        near_kernel,
        out_shape=jax.ShapeDtypeStruct((ENTRIES, 2 * BLK), F32),
        compiler_params=params(16),
        name="near_sums",
    )(own_ids, *pieces)


def second_kernel(own_ids, chosen, packed, near, feats, *rest):
    margins, pieces, (out, slots) = rest[:4], rest[4:8], rest[8:]
    acc = near[...] + sum_pieces(own_ids, pieces)
    w = chosen[...]
    w = w - STEP_SIZE * (acc[:, :BLK] + FIXED_RIDGE * w) / (acc[:, BLK:] + 1.0)
    ones = jnp.ones((BLK, 128), BF16)
    feature = lax.axis_index("feature")
    for shift, margin in zip(RING, margins):
        source = lax.rem(feature + FEATURES - shift, FEATURES)
        slots[pl.ds(source * 4, 4), :] = margin[TILES : TILES + 4, :]
    slot = slots[...].astype(I32)
    column = (slot % CAP + CAP * (iota((TILES, TILE), 0) // 4)).astype(F32).T
    owner = slot // CAP
    result = None
    lanes = (iota((TILE, 128), 1) % 32).astype(F32)
    for t in range(0, TILES, 2):
        both = [tile_margin(feats, w, t), tile_margin(feats, w, t + 1)]
        margin = sum_pieces_of([dot(p, ones) for p in split(jnp.concatenate(both, axis=0), 2)])
        place = [
            lanes == jnp.broadcast_to(column[:, q : q + 1], (TILE, 128)) for q in (t, t + 1)
        ]
        placed = jnp.where(jnp.concatenate(place, axis=0), margin, 0.0)
        owners = jnp.concatenate([owner[t : t + 1, :], owner[t + 1 : t + 2, :]], axis=1)
        mask = onehot(iota((DEVICES, 2 * TILE), 0) == owners).astype(BF16)
        term = sum_pieces_of([dot(mask, p) for p in split(placed, 2)])
        result = term if result is None else result + term
    out[...] = packed[...]
    result = jnp.where(iota((DEVICES, 128), 1) < 32, result, 0.0)
    for d in range(DEVICES):
        at = NOTE * d + CAP
        out[at : at + 1, :] = packed[at : at + 1, :] + result[d : d + 1, :]


def second_margin(near, pieces, own_ids, chosen, margins, packed, feats):
    return pl.pallas_call(
        second_kernel,
        in_specs=[VMEM] * 13,
        out_shape=jax.ShapeDtypeStruct((DEVICES * NOTE, 128), F32),
        scratch_shapes=[
            pltpu.VMEM((TILES, TILE), F32),
        ],
        compiler_params=params(16),
        name="second_margin",
    )(own_ids, chosen, packed, near, feats, *margins, *pieces)


def gathered_place(source):
    me = lax.axis_index("sample")
    x, z, core = me // 8, (me // 2) % 4, me % 2
    xs, zs, cs = source // 8, (source // 2) % 4, source % 2
    along_x, along_z = (x - xs + 4) % 4, (z - zs + 4) % 4
    late = jnp.where(cs == 0, along_x, along_z)
    early = jnp.where(cs == 0, along_z, along_x)
    return jnp.where(cs == core, 0, 16) + late * 4 + early


def weights_kernel(weights, *rest):
    pieces, rest = rest[:8], rest[8:]
    out, held, grad, hess, sent, table, ids, in_sems, out_sems, piece_sems, id_sem = rest
    blocks = weights.shape[0]
    arrivals = [
        pltpu.make_async_copy(piece, sent.at[pl.ds(4 * PACKET * i, 4 * PACKET)], piece_sems.at[i])
        for i, piece in enumerate(pieces)
    ]
    for copy in arrivals:
        copy.start()
    copies = fetch(weights, held, in_sems)

    def clear(i, carry):
        at = pl.ds(pl.multiple_of(i * 256, 256), 256)
        grad[at, :] = jnp.zeros((256, BLK), F32)
        hess[at, :] = jnp.zeros((256, BLK), F32)
        return carry

    lax.fori_loop(0, blocks // 256, clear, 0)
    for copy in arrivals:
        copy.wait()

    lines = [sent[i * PACKET + ENTRIES : i * PACKET + ENTRIES + 1, 0:128] for i in range(SAMPLES)]
    table[...] = jnp.concatenate(lines, axis=0).astype(I32)
    copy = pltpu.make_async_copy(table, ids, id_sem)
    copy.start()
    copy.wait()

    def source(s, carry):
        at = gathered_place(s)
        packet = sent.at[pl.ds(pl.multiple_of(at * PACKET, 8), PACKET)]
        for first in range(0, ENTRIES, 16):
            span = range(first, first + 16)
            rows = [pl.ds(ids[at, j], 1) for j in span]
            old = [(grad[r, :], hess[r, :]) for r in rows]
            new = [
                (g + packet[j : j + 1, 0:BLK], h + packet[j : j + 1, BLK : 2 * BLK])
                for j, (g, h) in zip(span, old)
            ]
            for r, (g, h) in zip(rows, new):
                grad[r, :] = g
                hess[r, :] = h
        return carry

    lax.fori_loop(0, SAMPLES, source, 0)
    size = blocks // CHUNKS
    done = []
    for c in range(CHUNKS):
        copies[c].wait()

        def update(i, carry, c=c):
            at = pl.ds(pl.multiple_of(c * size + i * 256, 256), 256)
            w = held[at, :]
            held[at, :] = w - STEP_SIZE * (grad[at, :] + FIXED_RIDGE * w) / (hess[at, :] + 1.0)
            return carry

        lax.fori_loop(0, size // 256, update, 0)
        at = pl.ds(c * size, size)
        copy = pltpu.make_async_copy(held.at[at], out.at[at], out_sems.at[c])
        copy.start()
        done.append(copy)
    for copy in done:
        copy.wait()


def all_weights(pieces, weights):
    blocks = weights.shape[0]
    return pl.pallas_call(
        weights_kernel,
        in_specs=[HBM] + [ANY] * 8,
        out_specs=HBM,
        out_shape=jax.ShapeDtypeStruct((blocks, BLK), F32),
        scratch_shapes=[
            pltpu.VMEM((blocks, BLK), F32),
            pltpu.VMEM((blocks + 8, BLK), F32),
            pltpu.VMEM((blocks + 8, BLK), F32),
            pltpu.VMEM((SAMPLES * PACKET, 2 * BLK), F32),
            pltpu.VMEM((SAMPLES, 128), I32),
            pltpu.SMEM((SAMPLES, 128), I32),
            pltpu.SemaphoreType.DMA((CHUNKS,)),
            pltpu.SemaphoreType.DMA((CHUNKS,)),
            pltpu.SemaphoreType.DMA((8,)),
            pltpu.SemaphoreType.DMA,
        ],
        compiler_params=params(WIDE),
        name="all_weights",
    )(weights, *pieces)


def pack_kernel(margin, members, labels, feats, out, slot, placed):
    feature = lax.axis_index("feature")
    slots = margin[TILES : TILES + 4, :].astype(I32)
    own = labels[pl.ds(feature * 4, 4), :]
    local = (members[...] % MEM + 1).astype(F32)
    columns = jnp.concatenate([(slots % CAP).astype(F32), own, local], axis=0).T
    lane = iota((TILE, 128), 1)
    within = (lane % CAP).astype(F32)
    for a in range(4):
        slot[:, a * TILE : (a + 1) * TILE] = slots[a : a + 1, :]
        rank, label, member = (
            jnp.broadcast_to(columns[:, 4 * q + a : 4 * q + a + 1], (TILE, 128)) for q in range(3)
        )
        value = jnp.where(lane // CAP == 4, label, jnp.where(lane // CAP == 5, member, 0.0))
        placed[a * TILE : (a + 1) * TILE, :] = jnp.where(within == rank, value, 0.0)
    line = slot[...]
    rows = dot_right(onehot(iota((POS, OWN), 0) == line).astype(BF16), feats[...], 3)
    notes = dot_right(onehot(iota((DEVICES, OWN), 0) == line // CAP).astype(BF16), placed[...], 3)
    for d in range(DEVICES):
        out[NOTE * d : NOTE * d + CAP, :] = rows[CAP * d : CAP * (d + 1), :]
        out[NOTE * d + CAP : NOTE * (d + 1), :] = notes[d : d + 1, :]


def pack_rows(margin, members, labels, feats):
    return pl.pallas_call(
        pack_kernel,
        out_shape=[
            jax.ShapeDtypeStruct((DEVICES * NOTE, 128), F32),
            jax.ShapeDtypeStruct((1, OWN), I32),
        ],
        scratch_shapes=[pltpu.VMEM((OWN, 128), F32)],
        compiler_params=params(16),
        name="pack_rows",
    )(margin, members, labels, feats)


def gram_times(gram, v):
    out = None
    for i in range(GROUP):
        term = gram[i] * v[i : i + 1, :]
        out = term if out is None else out + term
    return out


def spread(block, source):
    group = iota(block.shape, 1) // MEM
    out = None
    for g in range(4):
        shift = (g - source) % 4
        moved = pltpu.roll(block, MEM * shift, 1) if shift else block
        out = moved if out is None else jnp.where(group == g, moved, out)
    return out


def unpack(rows, feats, notes=None):
    for d in range(DEVICES):
        feats[CAP * d : CAP * (d + 1), :] = rows[NOTE * d : NOTE * d + CAP, :]
        if notes is not None:
            notes[d : d + 1, :] = rows[NOTE * d + CAP : NOTE * (d + 1), :]


def repeat_lanes(x, first, size):
    lane = iota(x.shape, 1)
    x = jnp.where((lane >= first) & (lane < first + size), x, 0.0)
    while size < 128:
        x = x + pltpu.roll(x, size, 1)
        size *= 2
    return x


def owner_kernel(rows, coefs, back, steps, lines, turned, diag, gram, work, held, notes):
    unpack(rows, held, notes)
    sub, lane = iota((128, 128), 0), iota((128, 128), 1)
    lab_parts, mem_parts, fixed_parts = [], [], []
    labs = repeat_lanes(notes[...], 4 * CAP, CAP)
    mems = repeat_lanes(notes[...], 5 * CAP, CAP)
    got = repeat_lanes(notes[...], 0, 32)
    for b in range(8):
        at = slice(16 * b, 16 * (b + 1))
        keep = iota((16, 128), 0) == iota((16, 128), 1) // CAP
        lab_parts.append(jnp.sum(jnp.where(keep, labs[at, :], 0.0), axis=0, keepdims=True))
        mem_parts.append(jnp.sum(jnp.where(keep, mems[at, :], 0.0), axis=0, keepdims=True))
        keep = iota((16, 128), 0) // FEATURES == iota((16, 128), 1) // 32
        fixed_parts.append(jnp.sum(jnp.where(keep, got[at, :], 0.0), axis=0, keepdims=True))
    lab = jnp.concatenate(lab_parts, axis=1)
    fixed = jnp.concatenate(fixed_parts, axis=1)
    mem = jnp.concatenate(mem_parts, axis=1).astype(I32) - 1
    few = onehot(iota((MEM, POS), 0) == mem)
    before = onehot(sub < lane).astype(BF16)
    ones = jnp.ones((128, 128), BF16)
    carry = jnp.zeros((MEM, 128), F32)
    ranks = []
    for b in range(8):
        part = few[:, 128 * b : 128 * (b + 1)]
        half = part.astype(BF16)
        count = dot(half, before) + carry
        carry = carry + dot(half, ones)
        ranks.append(jnp.sum(part * count, axis=0, keepdims=True))
    rnk = jnp.concatenate(ranks, axis=1).astype(I32)
    lines[0:8, :] = jnp.broadcast_to(mem, (8, POS))
    lines[8:16, :] = jnp.broadcast_to(rnk, (8, POS))
    by_rank = onehot((iota((GROUP, POS), 0) == rnk) & (mem >= 0))
    by_member = onehot((iota((128, POS), 0) % MEM) == mem).astype(BF16)
    y, offset, alive = dot_left(
        [(by_rank * lab, 3), (by_rank * fixed, 2), (by_rank, 1)], by_member, NT
    )
    target = jnp.where(mem >= 0, rnk * MEM + mem, -1)
    feats = held[...].T
    pieces = jnp.concatenate(split(feats, 2), axis=0)
    for b in range(4):
        goal = onehot(iota((256, POS), 0) + 256 * b == target).astype(BF16)
        moved = dot(pieces, goal, NT)
        turned[0, :, 256 * b : 256 * (b + 1)] = moved[0:128, :] + moved[128:256, :]
    x = turned[0]
    for p in range(1, 4):
        turned[p] = pltpu.roll(x, POS - MEM * p, 1)
    c = jnp.concatenate([coefs[...]] * 4, axis=0).T
    own = jnp.sum(x * jnp.concatenate([c] * 8, axis=1), axis=0, keepdims=True)
    own = jnp.where(iota((GROUP, POS), 1) // MEM == iota((GROUP, POS), 0), own, 0.0)
    folded = own[:, 0:128]
    for b in range(1, 8):
        folded = folded + own[:, 128 * b : 128 * (b + 1)]
    folded = folded + pltpu.roll(folded, 64, 1)
    s = folded + pltpu.roll(folded, 32, 1)
    for b in range(8):
        block = turned[0, :, 128 * b : 128 * (b + 1)]
        for delta in range(GROUP // 2 + 1):
            p, o = delta % 4, (b + delta // 4) % 8
            prod = block * turned[p, :, 128 * o : 128 * (o + 1)]
            diag[delta : delta + 1, 128 * b : 128 * (b + 1)] = jnp.sum(prod, axis=0, keepdims=True)
    for delta in range(GROUP // 2 + 1, GROUP):
        diag[delta : delta + 1, :] = pltpu.roll(
            jnp.broadcast_to(diag[GROUP - delta : GROUP - delta + 1, :], (8, POS)), POS - MEM * delta, 1
        )[0:1, :]
    for b in range(8):
        block = diag[:, 128 * b : 128 * (b + 1)]
        for p in range(4):
            i = 4 * b + p
            wide = spread(block, p)
            gram[i] = pltpu.roll(wide, i, 0) if i else wide
    at = iota((GROUP, 128), 0)
    steps_total = None
    for sweep in range(2):
        p = jax.nn.sigmoid(s + offset)
        error = (p - y) * alive
        d = jnp.sqrt(p * (1.0 - p) * alive)
        b = d * (gram_times(gram, error) + s)
        def formed(i):
            row = gram[i] * (d * d[i : i + 1, :])
            cut = i // 8 * 8
            one = row[cut : cut + 8, :] + onehot(iota((8, 128), 0) == i - cut)
            return jnp.concatenate(
                [row[r : r + 8, :] if r != cut else one for r in range(0, GROUP, 8)], axis=0
            )

        for k in range(0, GROUP, PIVOTS):
            panel = [work[k + q] if k else formed(q) for q in range(PIVOTS)]
            taken = []
            for q in range(PIVOTS):
                row = panel[q]
                inverse = 1.0 / row[k + q : k + q + 1, :]
                scaled = jnp.where(at == k + q, 1.0 - inverse, row * inverse)
                for r in range(q + 1, PIVOTS):
                    panel[r] = panel[r] - row[k + r : k + r + 1, :] * scaled
                b = b - b[k + q : k + q + 1, :] * scaled
                taken.append((row, scaled))
            for i in range(k + PIVOTS, GROUP):
                rest = work[i] if k else formed(i)
                for row, scaled in taken:
                    rest = rest - row[i : i + 1, :] * scaled
                work[i] = rest
        u = error - d * b
        s = s - MEMBER_STEP * (gram_times(gram, u) + MEMBER_RIDGE * s)
        steps_total = u * 0.25 if sweep == 0 else steps_total + u * 0.5
    steps[...] = steps_total
    final = (s + offset) * 0.25
    (scores,) = dot_left([(final, 2)], by_member)
    scores = jnp.sum(by_rank * scores, axis=0, keepdims=True)
    for b in range(8):
        line = jnp.broadcast_to(scores[:, 128 * b : 128 * (b + 1)], (16, 128))
        back[16 * b : 16 * (b + 1), :] = jnp.where(
            iota((16, 128), 1) // CAP == iota((16, 128), 0), line, 0.0
        )


def owner_work(rows, coefs):
    return pl.pallas_call(
        owner_kernel,
        out_shape=[
            jax.ShapeDtypeStruct((DEVICES, 128), F32),
            jax.ShapeDtypeStruct((GROUP, 128), F32),
            jax.ShapeDtypeStruct((16, POS), I32),
        ],
        scratch_shapes=[
            pltpu.VMEM((4, 128, POS), F32),
            pltpu.VMEM((GROUP, POS), F32),
            pltpu.VMEM((GROUP, GROUP, 128), F32),
            pltpu.VMEM((GROUP, GROUP, 128), F32),
            pltpu.VMEM((POS, 128), F32),
            pltpu.VMEM((DEVICES, 128), F32),
        ],
        compiler_params=params(WIDE),
        name="owner_work",
    )(rows, coefs)


def coefs_kernel(rows, coefs, steps, lines, out, held):
    unpack(rows, held)
    mem = lines[0:1, :]
    by_rank = onehot((iota((GROUP, POS), 0) == lines[8:9, :]) & (mem >= 0))
    by_member = onehot((iota((128, POS), 0) % MEM) == mem)
    (line,) = dot_left([(steps[...] * 0.25, 2)], by_member.astype(BF16))
    line = jnp.sum(by_rank * line, axis=0, keepdims=True)
    weighted = split(by_member[0:MEM, :] * line, 2)
    feats = split(held[...], 2)
    moved = dot(weighted[0], feats[0]) + dot(weighted[0], feats[1]) + dot(weighted[1], feats[0])
    out[...] = 0.25 * coefs[...] - moved


def new_coefs(rows, coefs, steps, lines):
    return pl.pallas_call(
        coefs_kernel,
        out_shape=jax.ShapeDtypeStruct((MEM, 128), F32),
        scratch_shapes=[pltpu.VMEM((POS, 128), F32)],
        compiler_params=params(16),
        name="new_coefs",
    )(rows, coefs, steps, lines)


def total_kernel(back, slots, out):
    slot = slots[...]
    mask = onehot(iota((DEVICES, OWN), 0) == slot // CAP).astype(BF16)
    (moved,) = dot_left([(back[...].T, 2)], mask)
    keep = (iota((128, OWN), 0) % CAP) == slot % CAP
    out[...] = jnp.sum(jnp.where(keep, moved, 0.0), axis=0, keepdims=True)


def total_rows(back, slots):
    return pl.pallas_call(
        total_kernel,
        out_shape=jax.ShapeDtypeStruct((1, OWN), F32),
        compiler_params=params(16),
        name="total_rows",
    )(back, slots)


def ring_feature(value):
    pairs = [[(i, (i + k) % FEATURES) for i in range(FEATURES)] for k in range(FEATURES)]
    return [value] + [lax.ppermute(value, "feature", pairs[k]) for k in RING[1:]]


def sample_pairs(shift, first):
    pairs = []
    for i in range(SAMPLES):
        x, z, core = i // 8, (i // 2) % 4, i % 2
        if (core == 0) == first:
            z = (z + shift) % 4
        else:
            x = (x + shift) % 4
        pairs.append((i, (x * 4 + z) * 2 + core))
    return pairs


def join_kernel(*refs):
    out = refs[-1]
    for i, ref in enumerate(refs[:-1]):
        out[i * PACKET : (i + 1) * PACKET, :] = ref[...]


def join(packets):
    return pl.pallas_call(
        join_kernel,
        out_shape=jax.ShapeDtypeStruct((len(packets) * PACKET, 2 * BLK), F32),
        compiler_params=params(16),
        name="join",
    )(*packets)


def gather_early(value):
    return join([value] + [lax.ppermute(value, "sample", sample_pairs(k, True)) for k in (1, 2, 3)])


def gather_late(early):
    late = [early] + [lax.ppermute(early, "sample", sample_pairs(k, False)) for k in (1, 2, 3)]
    other = [lax.ppermute(v, "sample", [(i, i ^ 1) for i in range(SAMPLES)]) for v in late]
    return late, other


def exchange(value):
    return lax.all_to_all(value, ("sample", "feature"), split_axis=0, concat_axis=0, tiled=True)


def shards(
    feat_values,
    block_ids,
    fixed_weights,
    labels,
    prior_scores,
    member_feats,
    member_ids,
    member_coefs,
):
    members = member_ids.reshape(4, TILE)
    label_tiles = labels.reshape(TILES, TILE)
    prior_tiles = prior_scores.reshape(TILES, TILE)
    ids = block_ids.T
    margin, chosen, held = first_margin(
        pltpu.with_memory_space_constraint(ids, pltpu.HBM),
        pltpu.with_memory_space_constraint(members, pltpu.HBM),
        feat_values,
        fixed_weights,
    )
    margin, ids = lax.optimization_barrier((margin, ids))
    own_ids, sent_ids, merge = block_tables(ids, fixed_weights.shape[0])
    margins = ring_feature(margin)
    packet = own_stats(margins, prior_tiles, label_tiles, sent_ids, merge, held)
    margin, packet = lax.optimization_barrier((margin, packet))
    packed, slot_row = pack_rows(margin, members, label_tiles, member_feats)
    early = gather_early(packet)
    early, packed = lax.optimization_barrier((early, packed))
    late, other = gather_late(early)
    near = near_sums(own_ids, late)
    message = second_margin(near, other, own_ids, chosen, margins, packed, held)
    rows = exchange(message.reshape(DEVICES, 1, NOTE * 128)).reshape(DEVICES * NOTE, 128)
    pieces = late + other
    weights = all_weights(pieces, fixed_weights)
    rows, weights = lax.optimization_barrier((rows, weights))
    back, steps, lines = owner_work(rows, member_coefs)
    returned = exchange(back[:, None, :])[:, 0, :]
    coefs = new_coefs(rows, member_coefs, steps, lines)
    total = total_rows(returned, slot_row)
    return (weights, coefs, total.reshape(OWN, 1))


def solution(mesh):
    both = ("sample", "feature")
    in_specs = (
        P("sample", "feature"),
        P("sample", "feature"),
        P("feature", None),
        P("sample"),
        P("sample"),
        P(both, None),
        P(both),
        P(both, None),
    )
    out_specs = (P("feature", None), P(both, None), P(both, None))
    return jax.shard_map(shards, mesh=mesh, in_specs=in_specs, out_specs=out_specs, check_vma=False)
```
